32 devices in a mesh: sec: 2 (over core), dom: 16 (over z, y, x).
Axes of the slice: x: 2, y: 2, z: 4, core: 2. Of those that a mesh axis runs over, the one named last changes fastest.
Arguments:
- state: float32 [3, 8, 262144], P(None, None, ('sec', 'dom')), may hold values from -6 to 6
- send_rows: int32 [524288], P(('sec', 'dom')), may hold values from 0 to 8191, as said below
- intersection_source: int32 [524288], P(('sec', 'dom')), may hold values from 0 to 16383, as said below
- intersection_weight: float32 [524288], P(('sec', 'dom')), may hold values from 0.1 to 1
- couple_rate: float32 [2, 3], P('sec'), may hold values from 0.2 to 0.8
- atm_metric: float32 [2, 131072], P(None, 'dom'), may hold values from 0.5 to 2
- wave_speed: float32 [8], replicated, may hold values from 0.5 to 2
- ocean_adjacent: int32 [6, 131072], P(None, 'dom'), may hold values from 0 to 9215, as said below
- ocean_edges: int32 [2, 8192], P(None, 'dom'), may hold values from 0 to 8191, as said below
- ocean_kappa: float32 [131072], P('dom'), may hold values from 0.02 to 0.15
Outputs:
- new_state: float32 [3, 8, 262144], P(None, None, ('sec', 'dom'))
The draws below stay inside these ranges and needn't reach their ends.
Inputs may be any that keep to these rules, and one draw needn't show every extreme that they name: `send_rows`: the ocean's band runs across the atmosphere's, so every block intersects every block of the other section. Within a block, cut the rows into 16 strips of 512 rows by position across the band; the 1024 slots for peer p hold the rows of strips p, p + 1, ... (modulo 16), 2 strips in all, in an order drawn from the seed; so every row fills exactly 2 slots. `intersection_source`: in each block a permutation of all 16384 received slots; the entries 2 * r .. 2 * r + 1 belong to row r. `ocean_adjacent`: each cell's neighbours on a hexagonal grid in its block's own row order; values from 8192 on name rim slots (first the cells of the previous block's last column, then those of the next block's first column, by position across the band); a cell at the band's edge names itself for a missing neighbour. `ocean_edges`: ordered by position across the band.
All inputs are finite; a program needn't handle non-finite values.
Results may differ from the reference program's by a relative error of at most 0.0001.
Values sent between devices are 32-bit elements; how exact they have to be, the bound alone decides.
A program may use at most 128 MiB of HBM per device.

```python
import math
import jax
import jax.numpy as jnp
import numpy as np
from jax import lax

LEV = 8
INTERSECTIONS = 2
XP = 16
YP = 512
ROWS = 8192
SLOTS = 16384
CAP = 1024
N_DOM = 16


def ocean_layout(key):
    base = jax.random.fold_in(key, 11)

    def one_device(device):
        order = jax.random.permutation(jax.random.fold_in(base, device), ROWS).astype(jnp.int32)
        places = jnp.zeros(ROWS, jnp.int32).at[order].set(jnp.arange(ROWS, dtype=jnp.int32))
        cells = jnp.arange(ROWS, dtype=jnp.int32)
        column = cells // YP
        height = cells % YP
        tilt = jnp.where(column % 2 == 1, 1, -1).astype(jnp.int32)
        zero_shift = jnp.zeros_like(cells)
        moves_x = [zero_shift, zero_shift, zero_shift + 1, zero_shift - 1, zero_shift + 1, zero_shift - 1]
        moves_y = [zero_shift + 1, zero_shift - 1, zero_shift, zero_shift, tilt, tilt]
        targets = []
        for moved_x, moved_y in zip(moves_x, moves_y):
            new_x = column + moved_x
            new_y = height + moved_y
            inside = (new_y >= 0) & (new_y < YP)
            safe_y = jnp.clip(new_y, 0, YP - 1)
            safe_x = jnp.clip(new_x, 0, XP - 1)
            local_row = places[safe_x * YP + safe_y]
            target = jnp.where(new_x < 0, ROWS + safe_y, jnp.where(new_x >= XP, ROWS + YP + safe_y, local_row))
            target = jnp.where(inside, target, places[cells])
            targets.append(target[order])
        positions = jnp.arange(YP, dtype=jnp.int32)
        edges = jnp.stack([places[positions], places[(XP - 1) * YP + positions]])
        return (jnp.stack(targets).astype(jnp.int32), edges.astype(jnp.int32), places)
    adjacency, edges, places = jax.vmap(one_device)(jnp.arange(N_DOM, dtype=jnp.int32))
    return (adjacency, edges, places)


def draw_ocean_adjacent(key, part):
    adjacency, edges, places = ocean_layout(key)
    return jnp.transpose(adjacency, (1, 0, 2)).reshape(6, N_DOM * ROWS)


def draw_ocean_edges(key, part):
    adjacency, edges, places = ocean_layout(key)
    return jnp.transpose(edges, (1, 0, 2)).reshape(2, N_DOM * YP)


def draw_send_rows(key, part):
    adjacency, edges, places = ocean_layout(key)
    base = jax.random.fold_in(key, 7)
    strip = ROWS // N_DOM
    order_ids = jnp.arange(ROWS, dtype=jnp.int32)
    crossing = order_ids % XP * YP + order_ids // XP

    def one_block(number):
        block_key = jax.random.fold_in(base, number)
        device = number % N_DOM
        lookup = jnp.where(number >= N_DOM, places[device], order_ids)
        listed = lookup[crossing]

        def one_peer(peer):
            shuffle = jax.random.permutation(jax.random.fold_in(block_key, peer), CAP).astype(jnp.int32)
            which = (peer + shuffle // strip) % N_DOM
            return listed[which * strip + shuffle % strip]
        return jax.vmap(one_peer)(jnp.arange(N_DOM, dtype=jnp.int32)).reshape(-1)
    return jax.vmap(one_block)(jnp.arange(2 * N_DOM, dtype=jnp.int32)).reshape(-1).astype(jnp.int32)


def draw_intersection_source(key, part):
    base = jax.random.fold_in(key, 5)

    def one_block(number):
        return jax.random.permutation(jax.random.fold_in(base, number), SLOTS).astype(jnp.int32)
    return jax.vmap(one_block)(jnp.arange(2 * N_DOM, dtype=jnp.int32)).reshape(-1)


def levels(stream_key, dims, pieces, least, top_value):
    loudness, own = 1.0, jax.random.fold_in(stream_key, 6)
    for dim, shards_of in pieces:
        draws = jnp.exp(jax.random.uniform(jax.random.fold_in(own, dim), (shards_of,), jnp.float32, least / len(pieces), top_value / len(pieces)))
        loudness = loudness * jnp.repeat(draws, dims[dim] // shards_of).reshape([-1 if axis == dim else 1 for axis in range(len(dims))])
    return loudness


def scatter_about(own_key, extent, scale, bound, split=(), kind=jnp.bfloat16):
    loudness = levels(own_key, extent, split, -0.22, 0.18) if split else 1.0
    values = jax.random.normal(own_key, extent, jnp.float32) * scale * loudness
    return jnp.minimum(jnp.maximum(values, -bound), bound).astype(kind)


def setup_inputs(seed: int = 0) -> dict:
    keys = jax.random.split(jax.random.key(seed), 11)
    return {
        "state": scatter_about(keys[0], (3, LEV, 2 * N_DOM * ROWS), 1.0, 6.0, ((2, 32),), jnp.float32),
        "send_rows": draw_send_rows(jax.random.fold_in(keys[10], 71), 0),
        "intersection_source": draw_intersection_source(jax.random.fold_in(keys[10], 71), 0),
        "intersection_weight": jnp.clip(jnp.exp(math.log(1.0) - 2.3025851 * jax.random.uniform(keys[3], (2 * N_DOM * INTERSECTIONS * ROWS,), jnp.float32) ** levels(keys[3], (2 * N_DOM * INTERSECTIONS * ROWS,), ((0, 32),), -0.2, 0.2)), 0.1, 1.0),
        "couple_rate": jnp.clip(0.2 + 0.6 * jax.random.uniform(keys[4], (2, 3), jnp.float32) ** levels(keys[4], (2, 3), ((0, 2),), -0.2, 0.2), 0.2, 0.8),
        "atm_metric": jnp.clip(jnp.exp(math.log(2.0) - 1.3862944 * jax.random.uniform(keys[5], (2, N_DOM * ROWS), jnp.float32) ** levels(keys[5], (2, N_DOM * ROWS), ((1, 16),), -0.2, 0.2)), 0.5, 2.0),
        "wave_speed": jnp.clip(jnp.exp(jax.random.uniform(keys[6], (LEV,), jnp.float32, math.log(0.5), math.log(2.0))), 0.5, 2.0),
        "ocean_adjacent": draw_ocean_adjacent(jax.random.fold_in(keys[10], 71), 0),
        "ocean_edges": draw_ocean_edges(jax.random.fold_in(keys[10], 71), 0),
        "ocean_kappa": jnp.clip(jnp.exp(math.log(0.15) - 2.014903 * jax.random.uniform(keys[9], (N_DOM * ROWS,), jnp.float32) ** levels(keys[9], (N_DOM * ROWS,), ((0, 16),), -0.2, 0.2)), 0.02, 0.15),
    }


TIME_STEP = 0.05

def gll_derivative():
    nodes = np.array([-1.0, -1.0 / np.sqrt(5.0), 1.0 / np.sqrt(5.0), 1.0])
    barycentric = np.array([1.0 / np.prod([nodes[first] - nodes[second] for second in range(4) if second != first]) for first in range(4)])
    matrix = np.zeros((4, 4))
    for first in range(4):
        for second in range(4):
            if first != second:
                matrix[first, second] = barycentric[second] / barycentric[first] / (nodes[first] - nodes[second])
        matrix[first, first] = -np.sum(matrix[first])
    return jnp.asarray(matrix, jnp.float32)

def along_first(field, derivative):
    depth, across, along = field.shape
    grouped = field.reshape(depth, across // 4, 4, along)
    return jnp.einsum('ij,lejy->leiy', derivative, grouped, precision=lax.Precision.HIGHEST).reshape(field.shape)

def along_second(field, derivative):
    depth, across, along = field.shape
    grouped = field.reshape(depth, across, along // 4, 4)
    return jnp.einsum('ij,lxej->lxei', derivative, grouped, precision=lax.Precision.HIGHEST).reshape(field.shape)

def dycore(fields, metric_x, metric_y, speeds):
    derivative = gll_derivative()
    eastward, northward, geopotential = (fields[0], fields[1], fields[2])
    slope_x = metric_x * along_first(geopotential, derivative)
    slope_y = metric_y * along_second(geopotential, derivative)
    spread = metric_x * along_first(eastward, derivative) + metric_y * along_second(northward, derivative)
    return jnp.stack([eastward - TIME_STEP * slope_x, northward - TIME_STEP * slope_y, geopotential - TIME_STEP * speeds[:, None, None] * spread])

def average_first(fields, before, after):
    phase = (jnp.arange(fields.shape[2]) % 4)[:, None]
    return jnp.where(phase == 3, (fields + after) * 0.5, jnp.where(phase == 0, (fields + before) * 0.5, fields))

def average_second(fields):
    along = fields.shape[3]
    position = jnp.arange(along)
    phase = position % 4
    after = jnp.roll(fields, -1, axis=3)
    before = jnp.roll(fields, 1, axis=3)
    joined_after = (phase == 3) & (position < along - 1)
    joined_before = (phase == 0) & (position > 0)
    return jnp.where(joined_after, (fields + after) * 0.5, jnp.where(joined_before, (fields + before) * 0.5, fields))

def reference(state, send_rows, intersection_source, intersection_weight, couple_rate, atm_metric, wave_speed, ocean_adjacent, ocean_edges, ocean_kappa):
    blocks = state.reshape(3, LEV, 2, N_DOM, ROWS)
    surface = blocks[:, LEV - 1]
    sender_rows = jnp.broadcast_to(send_rows.reshape(1, 2, N_DOM, SLOTS), (3, 2, N_DOM, SLOTS))
    outgoing = jnp.take_along_axis(surface, sender_rows, axis=3).reshape(3, 2, N_DOM, N_DOM, CAP)
    incoming = jnp.flip(outgoing, axis=1).transpose(0, 1, 3, 2, 4).reshape(3, 2, N_DOM, SLOTS)
    sources = jnp.broadcast_to(intersection_source.reshape(1, 2, N_DOM, INTERSECTIONS * ROWS), (3, 2, N_DOM, INTERSECTIONS * ROWS))
    values = jnp.take_along_axis(incoming, sources, axis=3).reshape(3, 2, N_DOM, ROWS, INTERSECTIONS)
    weights = intersection_weight.reshape(2, N_DOM, ROWS, INTERSECTIONS)
    regrid = lax.optimization_barrier(jnp.sum(values * weights, axis=-1)) / lax.optimization_barrier(jnp.sum(weights, axis=-1))
    atmosphere = blocks[:, :, 0].reshape(3, LEV, N_DOM * XP, YP)
    metric = atm_metric.reshape(2, N_DOM * XP, YP)
    stepped = dycore(atmosphere, metric[0], metric[1], wave_speed)
    averaged = average_second(average_first(stepped, jnp.roll(stepped, 1, axis=2), jnp.roll(stepped, -1, axis=2)))
    atmosphere_new = averaged.reshape(3, LEV, N_DOM, ROWS)
    ocean = blocks[:, :, 1]
    edges = ocean_edges.reshape(2, N_DOM, YP)
    left_values = jnp.take_along_axis(ocean, jnp.broadcast_to(edges[0], (3, LEV, N_DOM, YP)), axis=3)
    right_values = jnp.take_along_axis(ocean, jnp.broadcast_to(edges[1], (3, LEV, N_DOM, YP)), axis=3)
    extended = jnp.concatenate([ocean, jnp.roll(right_values, 1, axis=2), jnp.roll(left_values, -1, axis=2)], axis=3)
    adjacency = ocean_adjacent.reshape(6, N_DOM, ROWS)
    summed = jnp.zeros(ocean.shape, jnp.float32)
    for neighbor in range(6):
        gathered = jnp.take_along_axis(extended, jnp.broadcast_to(adjacency[neighbor], (3, LEV, N_DOM, ROWS)), axis=3)
        summed = summed + (gathered - ocean)
    ocean_new = ocean + ocean_kappa.reshape(N_DOM, ROWS) * summed
    updated = jnp.stack([atmosphere_new, ocean_new], axis=2)
    rates = couple_rate.T[:, :, None, None]
    surface_top = updated[:, LEV - 1]
    surface_top = surface_top + rates * (regrid - surface_top)
    updated = updated.at[:, LEV - 1].set(surface_top)
    return updated.reshape(3, LEV, 2 * N_DOM * ROWS)
```

```python
import functools
import jax
import jax.numpy as jnp
import numpy as np
from jax import lax
from jax.experimental import pallas as pl
from jax.experimental.pallas import tpu as pltpu
from jax.sharding import PartitionSpec as P

TIME_STEP = 0.05
LANES = 128
VMEM = pl.BlockSpec(memory_space=pltpu.VMEM)
SMEM = pl.BlockSpec(memory_space=pltpu.SMEM)
PARAMS = dict(vmem_limit_bytes=48 << 20)


def gll_derivative():
    nodes = np.array([-1.0, -1.0 / np.sqrt(5.0), 1.0 / np.sqrt(5.0), 1.0])
    barycentric = np.array(
        [1.0 / np.prod([nodes[i] - nodes[j] for j in range(4) if j != i]) for i in range(4)]
    )
    matrix = np.zeros((4, 4))
    for i in range(4):
        for j in range(4):
            if i != j:
                matrix[i, j] = barycentric[j] / barycentric[i] / (nodes[i] - nodes[j])
        matrix[i, i] = -np.sum(matrix[i])
    return matrix


DERIVATIVE = gll_derivative()


def two_terms(table):
    high = table.astype(jnp.bfloat16)
    low = (table - high.astype(jnp.float32)).astype(jnp.bfloat16)
    return jnp.concatenate([high, low], axis=1)


def pick(terms, depth, index):
    low = jnp.broadcast_to(index & (LANES - 1), (LANES, index.shape[1]))
    hot = (lax.broadcasted_iota(jnp.int32, low.shape, 0) == low).astype(jnp.float32).astype(jnp.bfloat16)
    found = jnp.dot(terms, jnp.concatenate([hot, hot], axis=0), preferred_element_type=jnp.float32)
    high = jnp.broadcast_to(index >> 7, (depth, index.shape[1]))
    own = lax.broadcasted_iota(jnp.int32, high.shape, 0) == high
    return [
        jnp.sum(jnp.where(own, found[f * depth : (f + 1) * depth], 0.0), axis=0, keepdims=True)
        for f in range(3)
    ]


def send_kernel(surface_ref, rows_ref, out_ref, terms_ref):
    depth = surface_ref.shape[1]
    for f in range(3):
        terms_ref[f * depth : (f + 1) * depth, :] = two_terms(surface_ref[f])
    per_peer = out_ref.shape[2]

    def step(i, _):
        index = jnp.concatenate([rows_ref[pl.ds(2 * i, 1), :], rows_ref[pl.ds(2 * i + 1, 1), :]], axis=1)
        values = pick(terms_ref[...], depth, index)
        for k in range(2):
            place = 2 * i + k
            for f in range(3):
                out_ref[place // per_peer, f, pl.ds(place % per_peer, 1), :] = values[f][
                    :, k * LANES : (k + 1) * LANES
                ]
        return 0

    lax.fori_loop(0, rows_ref.shape[0] // 2, step, 0)


def exchange_kernel(n, out_ref, in_ref, send_sem, recv_sem):
    sec, dom = lax.axis_index("sec"), lax.axis_index("dom")
    barrier = pltpu.get_barrier_semaphore()

    def greet(p, _):
        pl.semaphore_signal(barrier, inc=1, device_id=(1 - sec, p), device_id_type=pl.DeviceIdType.MESH)
        return 0

    lax.fori_loop(0, n, greet, 0)
    pl.semaphore_wait(barrier, n)

    def copy(k):
        p = lax.rem(dom + k, n)
        return pltpu.make_async_remote_copy(
            src_ref=out_ref.at[p],
            dst_ref=in_ref.at[dom],
            send_sem=send_sem.at[k],
            recv_sem=recv_sem.at[k],
            device_id=(1 - sec, p),
            device_id_type=pl.DeviceIdType.MESH,
        )

    def start(k, _):
        copy(k).start()
        return 0

    def wait(k, _):
        copy(k).wait()
        return 0

    lax.fori_loop(0, n, start, 0)
    lax.fori_loop(0, n, wait, 0)


def lane_phase(shape):
    return lax.broadcasted_iota(jnp.int32, shape, 1) % 4


def along_second(value, phase):
    width = value.shape[1]
    total = jnp.zeros_like(value)
    for shift in range(-3, 4):
        factor = jnp.zeros(value.shape, jnp.float32)
        for i in range(4):
            if 0 <= i + shift < 4:
                factor = jnp.where(phase == i, np.float32(DERIVATIVE[i, i + shift]), factor)
        moved = value if shift == 0 else pltpu.roll(value, (-shift) % width, 1)
        total = total + factor * moved
    return total


def advance_kernel(x_points, y_points, state_ref, metric_ref, speed_ref, stepped_ref):
    @pl.when(lax.axis_index("sec") == 0)
    def _():
        def piece(g, _):
            def at(i, f):
                return state_ref[f, :, pl.ds(pl.multiple_of(start + i * y_points, LANES), LANES)]

            start = (g // (y_points // LANES)) * 4 * y_points + (g % (y_points // LANES)) * LANES
            phase = lane_phase((state_ref.shape[1], LANES))
            u = [at(i, 0) for i in range(4)]
            v = [at(i, 1) for i in range(4)]
            h = [at(i, 2) for i in range(4)]
            speed = speed_ref[...]
            for i in range(4):
                here = pl.ds(pl.multiple_of(start + i * y_points, LANES), LANES)
                gx = metric_ref[0:1, here]
                gy = metric_ref[1:2, here]
                dx_h = sum(np.float32(DERIVATIVE[i, j]) * h[j] for j in range(4))
                dx_u = sum(np.float32(DERIVATIVE[i, j]) * u[j] for j in range(4))
                stepped_ref[0, :, here] = u[i] - TIME_STEP * (gx * dx_h)
                stepped_ref[1, :, here] = v[i] - TIME_STEP * (gy * along_second(h[i], phase))
                spread = gx * dx_u + gy * along_second(v[i], phase)
                stepped_ref[2, :, here] = h[i] - TIME_STEP * speed * spread
            return 0

        lax.fori_loop(0, x_points // 4 * (y_points // LANES), piece, 0)

    @pl.when(lax.axis_index("sec") == 1)
    def _():
        for f in range(3):
            stepped_ref[f] = state_ref[f]


def to_rows(source_ref, source_at, table_ref, table_at, count):
    def piece(c, _):
        here = pl.ds(pl.multiple_of(source_at + c * LANES, LANES), LANES)
        block = jnp.concatenate([source_ref[f, :, here] for f in range(3)], axis=0)
        fill = jnp.zeros((LANES - block.shape[0], LANES), jnp.float32)
        table_ref[pl.ds(pl.multiple_of(table_at + c * LANES, LANES), LANES), :] = jnp.transpose(
            jnp.concatenate([block, fill], axis=0)
        )
        return 0

    lax.fori_loop(0, count // LANES, piece, 0)


def from_rows(table_ref, at, levels):
    block = jnp.transpose(table_ref[pl.ds(pl.multiple_of(at, LANES), LANES), :])
    return [block[f * levels : (f + 1) * levels] for f in range(3)]


def edge_kernel(state_ref, edges_ref, border_ref, table_ref, picked_ref):
    rows = state_ref.shape[2]
    count = edges_ref.shape[0]
    to_rows(state_ref, 0, table_ref, 0, rows)

    def step(i, _):
        base = i * 16
        places = [edges_ref[base + u] for u in range(16)]
        for u in range(16):
            picked_ref[pl.ds(base + u, 1), :] = table_ref[pl.ds(places[u], 1), :]
        return 0

    lax.fori_loop(0, count // 16, step, 0)
    for c in range(count // LANES):
        block = from_rows(picked_ref, c * LANES, state_ref.shape[1])
        for f in range(3):
            border_ref[f, :, c * LANES : (c + 1) * LANES] = block[f]


def sweep_kernel(state_ref, west_ref, east_ref, adjacent_ref, kappa_ref, swept_ref, table_ref, sum_ref):
    levels, rows, edge = state_ref.shape[1], state_ref.shape[2], west_ref.shape[2]
    part = swept_ref.shape[2]
    to_rows(state_ref, 0, table_ref, 0, rows)
    to_rows(west_ref, 0, table_ref, rows, edge)
    to_rows(east_ref, 0, table_ref, rows + edge, edge)

    def step(i, _):
        base = i * 16
        places = [[adjacent_ref[base + (j * part + u)] for j in range(6)] for u in range(16)]
        for u in range(16):
            a = [table_ref[pl.ds(p, 1), :] for p in places[u]]
            sum_ref[pl.ds(base + u, 1), :] = ((a[0] + a[1]) + (a[2] + a[3])) + (a[4] + a[5])
        return 0

    lax.fori_loop(0, part // 16, step, 0)
    first = lax.axis_index("sec") * part

    def finish(c, _):
        here = pl.ds(pl.multiple_of(c * LANES, LANES), LANES)
        there = pl.ds(pl.multiple_of(first + c * LANES, LANES), LANES)
        block = from_rows(sum_ref, c * LANES, levels)
        kappa = kappa_ref[0:1, here]
        for f in range(3):
            value = state_ref[f, :, there]
            swept_ref[f, :, here] = value + kappa * (block[f] - 6.0 * value)
        return 0

    lax.fori_loop(0, part // LANES, finish, 0)


def deinterleave(values, offset):
    count = values.shape[0]
    i = lax.broadcasted_iota(jnp.int32, (LANES, LANES), 0)
    j = lax.broadcasted_iota(jnp.int32, (LANES, LANES), 1)
    m = lax.broadcasted_iota(jnp.int32, (count // 2, count), 0)
    q = lax.broadcasted_iota(jnp.int32, (count // 2, count), 1)
    total = jnp.zeros((count // 2, LANES), jnp.float32)
    for b in range(2):
        chosen = (i == 2 * (j - b * (LANES // 2)) + offset).astype(jnp.float32)
        packed = jnp.dot(
            values, chosen, preferred_element_type=jnp.float32, precision=lax.Precision.HIGHEST
        )
        gathered = (q == 2 * m + b).astype(jnp.float32)
        total = total + jnp.dot(
            gathered, packed, preferred_element_type=jnp.float32, precision=lax.Precision.HIGHEST
        )
    return total


def final_kernel(
    x_points, y_points, incoming_ref, source_ref, weight_ref, rate_ref, stepped_ref, west_ref, east_ref,
    own_ref, helped_ref, new_ref, terms_ref, index_ref, share_ref,
):
    atmosphere = lax.axis_index("sec") == 0
    levels = stepped_ref.shape[1]
    depth = source_ref.shape[0]

    @pl.when(atmosphere)
    def _():
        for f in range(3):
            for x in range(x_points):
                here = slice(x * y_points, (x + 1) * y_points)
                value = stepped_ref[f, :, here]
                if x % 4 == 3:
                    other = (
                        stepped_ref[f, :, (x + 1) * y_points : (x + 2) * y_points]
                        if x < x_points - 1
                        else east_ref[f]
                    )
                    value = (value + other) * 0.5
                elif x % 4 == 0:
                    other = stepped_ref[f, :, (x - 1) * y_points : x * y_points] if x else west_ref[f]
                    value = (value + other) * 0.5
                position = lax.broadcasted_iota(jnp.int32, value.shape, 1)
                phase = position % 4
                after = pltpu.roll(value, y_points - 1, 1)
                before = pltpu.roll(value, 1, 1)
                new_ref[f, :, here] = jnp.where(
                    (phase == 3) & (position < y_points - 1),
                    (value + after) * 0.5,
                    jnp.where((phase == 0) & (position > 0), (value + before) * 0.5, value),
                )

    @pl.when(jnp.logical_not(atmosphere))
    def _():
        part = own_ref.shape[2]
        for f in range(3):
            new_ref[f, :, :part] = helped_ref[f]
            new_ref[f, :, part:] = own_ref[f]

    for f in range(3):
        table = incoming_ref[:, f].reshape(depth, LANES)
        terms_ref[f * depth : (f + 1) * depth, :] = two_terms(table)
    source = source_ref[...].astype(jnp.float32)
    for k in range(2):
        index_ref[:, k * LANES : (k + 1) * LANES] = (deinterleave(source, k) + 0.5).astype(jnp.int32)
        share_ref[:, k * LANES : (k + 1) * LANES] = deinterleave(weight_ref[...], k)

    def step(c, _):
        values = pick(terms_ref[...], depth, index_ref[pl.ds(c, 1), :])
        weight = share_ref[pl.ds(c, 1), :]
        whole = weight[:, :LANES] + weight[:, LANES:]
        here = pl.ds(pl.multiple_of(c * LANES, LANES), LANES)
        for f in range(3):
            product = values[f] * weight
            regrid = (product[:, :LANES] + product[:, LANES:]) / whole
            top = new_ref[f, levels - 1 : levels, here]
            new_ref[f, levels - 1 : levels, here] = top + rate_ref[0, f] * (regrid - top)
        return 0

    lax.fori_loop(0, depth // 2, step, 0)


def body(
    state, send_rows, intersection_source, intersection_weight, couple_rate, atm_metric, wave_speed,
    ocean_adjacent, ocean_edges, ocean_kappa,
):
    levels, rows = state.shape[1], state.shape[2]
    y_points = ocean_edges.shape[1]
    x_points = rows // y_points
    n = lax.axis_size("dom")
    sec = lax.axis_index("sec")
    slots = send_rows.shape[0]
    cap = slots // n
    part = rows // 2
    f32 = jnp.float32

    ocean = lax.ppermute(state, "sec", [(1, 0)])
    ocean = jnp.where(sec == 0, ocean, state)

    surface = state[:, levels - 1].reshape(3, rows // LANES, LANES)
    outgoing = pl.pallas_call(
        send_kernel,
        out_shape=jax.ShapeDtypeStruct((n, 3, cap // LANES, LANES), f32),
        in_specs=[VMEM] * 2,
        out_specs=VMEM,
        scratch_shapes=[pltpu.VMEM((3 * rows // LANES, 2 * LANES), jnp.bfloat16)],
        compiler_params=pltpu.CompilerParams(**PARAMS),
        name="pick_sent",
    )(surface, send_rows.reshape(-1, LANES))
    incoming = pl.pallas_call(
        functools.partial(exchange_kernel, n),
        out_shape=jax.ShapeDtypeStruct(outgoing.shape, f32),
        in_specs=[VMEM],
        out_specs=VMEM,
        scratch_shapes=[
            pltpu.SemaphoreType.DMA((n,)),
            pltpu.SemaphoreType.DMA((n,)),
        ],
        compiler_params=pltpu.CompilerParams(collective_id=0, has_side_effects=True, **PARAMS),
        name="exchange",
    )(outgoing)

    stepped = pl.pallas_call(
        functools.partial(advance_kernel, x_points, y_points),
        out_shape=jax.ShapeDtypeStruct(state.shape, f32),
        in_specs=[VMEM] * 3,
        out_specs=VMEM,
        compiler_params=pltpu.CompilerParams(**PARAMS),
        name="advance",
    )(state, atm_metric, jnp.broadcast_to(wave_speed[:, None], (levels, LANES)))
    rim = pl.pallas_call(
        edge_kernel,
        out_shape=jax.ShapeDtypeStruct((3, levels, 2 * y_points), f32),
        in_specs=[VMEM, SMEM],
        out_specs=VMEM,
        scratch_shapes=[pltpu.VMEM((rows, LANES), f32), pltpu.VMEM((2 * y_points, LANES), f32)],
        compiler_params=pltpu.CompilerParams(**PARAMS),
        name="pick_edges",
    )(ocean, ocean_edges.reshape(-1))

    up = [(i, (i + 1) % n) for i in range(n)]
    down = [(j, i) for i, j in up]
    eastward = jnp.stack([stepped[:, :, rows - y_points :], rim[:, :, y_points:]])
    westward = jnp.stack([stepped[:, :, :y_points], rim[:, :, :y_points]])
    west = lax.ppermute(eastward, "dom", up)
    east = lax.ppermute(westward, "dom", down)

    adjacent = lax.dynamic_slice_in_dim(ocean_adjacent, sec * part, part, 1).reshape(-1)
    kappa = lax.dynamic_slice_in_dim(ocean_kappa, sec * part, part, 0).reshape(1, -1)
    swept = pl.pallas_call(
        sweep_kernel,
        out_shape=jax.ShapeDtypeStruct((3, levels, part), f32),
        in_specs=[VMEM] * 3 + [SMEM, VMEM],
        out_specs=VMEM,
        scratch_shapes=[
            pltpu.VMEM((rows + 2 * y_points, LANES), f32),
            pltpu.VMEM((part, LANES), f32),
        ],
        compiler_params=pltpu.CompilerParams(**PARAMS),
        name="sweep",
    )(ocean, west[1], east[1], adjacent, kappa)
    helped = lax.ppermute(swept, "sec", [(0, 1)])

    return pl.pallas_call(
        functools.partial(final_kernel, x_points, y_points),
        out_shape=jax.ShapeDtypeStruct(state.shape, f32),
        in_specs=[VMEM] * 3 + [SMEM] + [VMEM] * 5,
        out_specs=VMEM,
        scratch_shapes=[
            pltpu.VMEM((3 * slots // LANES, 2 * LANES), jnp.bfloat16),
            pltpu.VMEM((slots // LANES // 2, 2 * LANES), jnp.int32),
            pltpu.VMEM((slots // LANES // 2, 2 * LANES), f32),
        ],
        compiler_params=pltpu.CompilerParams(**PARAMS),
        name="finish",
    )(
        incoming,
        intersection_source.reshape(-1, LANES),
        intersection_weight.reshape(-1, LANES),
        couple_rate,
        stepped,
        west[0],
        east[0],
        swept,
        helped,
    )


def solution(mesh):
    in_specs = (
        P(None, None, ("sec", "dom")),
        P(("sec", "dom")),
        P(("sec", "dom")),
        P(("sec", "dom")),
        P("sec", None),
        P(None, "dom"),
        P(),
        P(None, "dom"),
        P(None, "dom"),
        P("dom"),
    )
    out_specs = P(None, None, ("sec", "dom"))
    return jax.shard_map(body, mesh=mesh, in_specs=in_specs, out_specs=out_specs, check_vma=False)
```

```python
import functools
import jax
import jax.numpy as jnp
import numpy as np
from jax import lax
from jax.experimental import pallas as pl
from jax.experimental.pallas import tpu as pltpu
from jax.sharding import PartitionSpec as P

TIME_STEP = 0.05
LANES = 128
VMEM = pl.BlockSpec(memory_space=pltpu.VMEM)
SMEM = pl.BlockSpec(memory_space=pltpu.SMEM)
PARAMS = dict(vmem_limit_bytes=48 << 20)


def gll_derivative():
    nodes = np.array([-1.0, -1.0 / np.sqrt(5.0), 1.0 / np.sqrt(5.0), 1.0])
    barycentric = np.array(
        [1.0 / np.prod([nodes[i] - nodes[j] for j in range(4) if j != i]) for i in range(4)]
    )
    matrix = np.zeros((4, 4))
    for i in range(4):
        for j in range(4):
            if i != j:
                matrix[i, j] = barycentric[j] / barycentric[i] / (nodes[i] - nodes[j])
        matrix[i, i] = -np.sum(matrix[i])
    return matrix


DERIVATIVE = gll_derivative()


def two_terms(table):
    high = table.astype(jnp.bfloat16)
    low = (table - high.astype(jnp.float32)).astype(jnp.bfloat16)
    return jnp.concatenate([high, low], axis=1)


def pick(terms, depth, index):
    low = jnp.broadcast_to(index & (LANES - 1), (LANES, index.shape[1]))
    hot = (lax.broadcasted_iota(jnp.int32, low.shape, 0) == low).astype(jnp.float32).astype(jnp.bfloat16)
    found = jnp.dot(terms, jnp.concatenate([hot, hot], axis=0), preferred_element_type=jnp.float32)
    high = jnp.broadcast_to(index >> 7, (depth, index.shape[1]))
    own = lax.broadcasted_iota(jnp.int32, high.shape, 0) == high
    return [
        jnp.sum(jnp.where(own, found[f * depth : (f + 1) * depth], 0.0), axis=0, keepdims=True)
        for f in range(3)
    ]


def send_kernel(surface_ref, rows_ref, out_ref, terms_ref):
    depth = surface_ref.shape[1]
    for f in range(3):
        terms_ref[f * depth : (f + 1) * depth, :] = two_terms(surface_ref[f])
    per_peer = out_ref.shape[2]

    def step(i, _):
        index = jnp.concatenate([rows_ref[pl.ds(2 * i, 1), :], rows_ref[pl.ds(2 * i + 1, 1), :]], axis=1)
        values = pick(terms_ref[...], depth, index)
        for k in range(2):
            place = 2 * i + k
            for f in range(3):
                out_ref[place // per_peer, f, pl.ds(place % per_peer, 1), :] = values[f][
                    :, k * LANES : (k + 1) * LANES
                ]
        return 0

    lax.fori_loop(0, rows_ref.shape[0] // 2, step, 0, unroll=4)


def exchange_kernel(
    n, out_ref, stepped_ref, rim_ref, in_ref, west_a_ref, east_a_ref, west_o_ref, east_o_ref,
    send_sem, recv_sem, edge_send_sem, edge_recv_sem,
):
    sec, dom = lax.axis_index("sec"), lax.axis_index("dom")
    right, left = lax.rem(dom + 1, n), lax.rem(dom + n - 1, n)
    mesh_ids = pl.DeviceIdType.MESH
    barrier = pltpu.get_barrier_semaphore()

    def greet(p, _):
        pl.semaphore_signal(barrier, inc=1, device_id=(1 - sec, p), device_id_type=mesh_ids)
        return 0

    lax.fori_loop(0, n, greet, 0)
    for side in (left, right):
        pl.semaphore_signal(barrier, inc=1, device_id=(sec, side), device_id_type=mesh_ids)
    pl.semaphore_wait(barrier, n + 2)

    edge, rows = west_a_ref.shape[2], stepped_ref.shape[2]
    first, last = pl.ds(0, edge), pl.ds(rows - edge, edge)
    edges = []
    for k, (source, target, side) in enumerate(
        (
            (rim_ref.at[:, :, pl.ds(edge, edge)], west_o_ref, right),
            (rim_ref.at[:, :, first], east_o_ref, left),
            (stepped_ref.at[:, :, last], west_a_ref, right),
            (stepped_ref.at[:, :, first], east_a_ref, left),
        )
    ):
        edges.append(
            pltpu.make_async_remote_copy(
                src_ref=source,
                dst_ref=target,
                send_sem=edge_send_sem.at[k],
                recv_sem=edge_recv_sem.at[k],
                device_id=(sec, side),
                device_id_type=mesh_ids,
            )
        )

    def copy(k):
        p = lax.rem(dom + k, n)
        return pltpu.make_async_remote_copy(
            src_ref=out_ref.at[p],
            dst_ref=in_ref.at[dom],
            send_sem=send_sem.at[k],
            recv_sem=recv_sem.at[k],
            device_id=(1 - sec, p),
            device_id_type=mesh_ids,
        )

    def start(k, _):
        copy(k).start()
        return 0

    def wait(k, _):
        copy(k).wait()
        return 0

    for each in edges:
        each.start()
    lax.fori_loop(0, n, start, 0)
    lax.fori_loop(0, n, wait, 0)
    for each in edges:
        each.wait()


def lane_phase(shape):
    return lax.broadcasted_iota(jnp.int32, shape, 1) % 4


def along_second(value, phase):
    width = value.shape[1]
    total = jnp.zeros_like(value)
    for shift in range(-3, 4):
        factor = jnp.zeros(value.shape, jnp.float32)
        for i in range(4):
            if 0 <= i + shift < 4:
                factor = jnp.where(phase == i, np.float32(DERIVATIVE[i, i + shift]), factor)
        moved = value if shift == 0 else pltpu.roll(value, (-shift) % width, 1)
        total = total + factor * moved
    return total


def advance_kernel(x_points, y_points, state_ref, metric_ref, speed_ref, stepped_ref):
    @pl.when(lax.axis_index("sec") == 0)
    def _():
        def piece(g, _):
            def at(i, f):
                return state_ref[f, :, pl.ds(pl.multiple_of(start + i * y_points, LANES), LANES)]

            start = (g // (y_points // LANES)) * 4 * y_points + (g % (y_points // LANES)) * LANES
            phase = lane_phase((state_ref.shape[1], LANES))
            u = [at(i, 0) for i in range(4)]
            v = [at(i, 1) for i in range(4)]
            h = [at(i, 2) for i in range(4)]
            speed = speed_ref[...]
            for i in range(4):
                here = pl.ds(pl.multiple_of(start + i * y_points, LANES), LANES)
                gx = metric_ref[0:1, here]
                gy = metric_ref[1:2, here]
                dx_h = sum(np.float32(DERIVATIVE[i, j]) * h[j] for j in range(4))
                dx_u = sum(np.float32(DERIVATIVE[i, j]) * u[j] for j in range(4))
                stepped_ref[0, :, here] = u[i] - TIME_STEP * (gx * dx_h)
                stepped_ref[1, :, here] = v[i] - TIME_STEP * (gy * along_second(h[i], phase))
                spread = gx * dx_u + gy * along_second(v[i], phase)
                stepped_ref[2, :, here] = h[i] - TIME_STEP * speed * spread
            return 0

        lax.fori_loop(0, x_points // 4 * (y_points // LANES), piece, 0)

    @pl.when(lax.axis_index("sec") == 1)
    def _():
        for f in range(3):
            stepped_ref[f] = state_ref[f]


def to_rows(source_ref, source_at, table_ref, table_at, count):
    def piece(c, _):
        here = pl.ds(pl.multiple_of(source_at + c * LANES, LANES), LANES)
        block = jnp.concatenate([source_ref[f, :, here] for f in range(3)], axis=0)
        there = pl.ds(pl.multiple_of(table_at + c * LANES, LANES), LANES)
        table_ref[there, : block.shape[0]] = jnp.transpose(block)
        return 0

    lax.fori_loop(0, count // LANES, piece, 0, unroll=4)


def from_rows(table_ref, at, levels):
    block = jnp.transpose(table_ref[pl.ds(pl.multiple_of(at, LANES), LANES), :])
    return [block[f * levels : (f + 1) * levels] for f in range(3)]


def edge_kernel(state_ref, edges_ref, border_ref, table_ref, picked_ref):
    rows = state_ref.shape[2]
    count = edges_ref.shape[0]
    to_rows(state_ref, 0, table_ref, 0, rows)

    def step(i, _):
        base = i * 16
        places = [edges_ref[base + u] for u in range(16)]
        for u in range(16):
            picked_ref[pl.ds(base + u, 1), :] = table_ref[pl.ds(places[u], 1), :]
        return 0

    lax.fori_loop(0, count // 16, step, 0)
    for c in range(count // LANES):
        block = from_rows(picked_ref, c * LANES, state_ref.shape[1])
        for f in range(3):
            border_ref[f, :, c * LANES : (c + 1) * LANES] = block[f]


def sweep_kernel(state_ref, west_ref, east_ref, adjacent_ref, kappa_ref, swept_ref, table_ref, sum_ref):
    levels, rows, edge = state_ref.shape[1], state_ref.shape[2], west_ref.shape[2]
    part = swept_ref.shape[2]
    to_rows(state_ref, 0, table_ref, 0, rows)
    to_rows(west_ref, 0, table_ref, rows, edge)
    to_rows(east_ref, 0, table_ref, rows + edge, edge)

    def step(i, _):
        base = i * 16
        places = [[adjacent_ref[base + (j * part + u)] for j in range(6)] for u in range(16)]
        for u in range(16):
            a = [table_ref[pl.ds(p, 1), :] for p in places[u]]
            sum_ref[pl.ds(base + u, 1), :] = ((a[0] + a[1]) + (a[2] + a[3])) + (a[4] + a[5])
        return 0

    lax.fori_loop(0, part // 16, step, 0)
    first = lax.axis_index("sec") * part

    def finish(c, _):
        here = pl.ds(pl.multiple_of(c * LANES, LANES), LANES)
        there = pl.ds(pl.multiple_of(first + c * LANES, LANES), LANES)
        block = from_rows(sum_ref, c * LANES, levels)
        kappa = kappa_ref[0:1, here]
        for f in range(3):
            value = state_ref[f, :, there]
            swept_ref[f, :, here] = value + kappa * (block[f] - 6.0 * value)
        return 0

    lax.fori_loop(0, part // LANES, finish, 0, unroll=4)


def deinterleave(values, offset):
    count = values.shape[0]
    i = lax.broadcasted_iota(jnp.int32, (LANES, LANES), 0)
    j = lax.broadcasted_iota(jnp.int32, (LANES, LANES), 1)
    m = lax.broadcasted_iota(jnp.int32, (count // 2, count), 0)
    q = lax.broadcasted_iota(jnp.int32, (count // 2, count), 1)
    total = jnp.zeros((count // 2, LANES), jnp.float32)
    for b in range(2):
        chosen = (i == 2 * (j - b * (LANES // 2)) + offset).astype(jnp.float32)
        packed = jnp.dot(
            values, chosen, preferred_element_type=jnp.float32, precision=lax.Precision.HIGHEST
        )
        gathered = (q == 2 * m + b).astype(jnp.float32)
        total = total + jnp.dot(
            gathered, packed, preferred_element_type=jnp.float32, precision=lax.Precision.HIGHEST
        )
    return total


def regrid_kernel(incoming_ref, source_ref, weight_ref, regrid_ref, terms_ref, index_ref, share_ref):
    depth = source_ref.shape[0]
    for f in range(3):
        table = incoming_ref[:, f].reshape(depth, LANES)
        terms_ref[f * depth : (f + 1) * depth, :] = two_terms(table)
    source = source_ref[...].astype(jnp.float32)
    for k in range(2):
        index_ref[:, k * LANES : (k + 1) * LANES] = (deinterleave(source, k) + 0.5).astype(jnp.int32)
        share_ref[:, k * LANES : (k + 1) * LANES] = deinterleave(weight_ref[...], k)

    def step(c, _):
        values = pick(terms_ref[...], depth, index_ref[pl.ds(c, 1), :])
        weight = share_ref[pl.ds(c, 1), :]
        whole = weight[:, :LANES] + weight[:, LANES:]
        here = pl.ds(pl.multiple_of(c * LANES, LANES), LANES)
        for f in range(3):
            product = values[f] * weight
            regrid_ref[f : f + 1, here] = (product[:, :LANES] + product[:, LANES:]) / whole
        return 0

    lax.fori_loop(0, depth // 2, step, 0, unroll=4)


def finish_kernel(
    x_points, y_points, regrid_ref, rate_ref, stepped_ref, west_ref, east_ref, own_ref, helped_ref, new_ref,
):
    atmosphere = lax.axis_index("sec") == 0
    levels = stepped_ref.shape[1]

    def couple(f, here, value):
        rate = rate_ref[0, f]
        row = lax.broadcasted_iota(jnp.int32, value.shape, 0)
        relaxed = value + rate * (regrid_ref[f : f + 1, here] - value)
        new_ref[f, :, here] = jnp.where(row == levels - 1, relaxed, value)

    @pl.when(atmosphere)
    def _():
        for f in range(3):
            for x in range(x_points):
                here = slice(x * y_points, (x + 1) * y_points)
                value = stepped_ref[f, :, here]
                if x % 4 == 3:
                    other = (
                        stepped_ref[f, :, (x + 1) * y_points : (x + 2) * y_points]
                        if x < x_points - 1
                        else east_ref[f]
                    )
                    value = (value + other) * 0.5
                elif x % 4 == 0:
                    other = stepped_ref[f, :, (x - 1) * y_points : x * y_points] if x else west_ref[f]
                    value = (value + other) * 0.5
                position = lax.broadcasted_iota(jnp.int32, value.shape, 1)
                phase = position % 4
                after = pltpu.roll(value, y_points - 1, 1)
                before = pltpu.roll(value, 1, 1)
                averaged = jnp.where(
                    (phase == 3) & (position < y_points - 1),
                    (value + after) * 0.5,
                    jnp.where((phase == 0) & (position > 0), (value + before) * 0.5, value),
                )
                couple(f, here, averaged)

    @pl.when(jnp.logical_not(atmosphere))
    def _():
        part = own_ref.shape[2]
        for f in range(3):
            couple(f, slice(0, part), helped_ref[f])
            couple(f, slice(part, 2 * part), own_ref[f])


def body(
    state, send_rows, intersection_source, intersection_weight, couple_rate, atm_metric, wave_speed,
    ocean_adjacent, ocean_edges, ocean_kappa,
):
    levels, rows = state.shape[1], state.shape[2]
    y_points = ocean_edges.shape[1]
    x_points = rows // y_points
    n = lax.axis_size("dom")
    sec = lax.axis_index("sec")
    slots = send_rows.shape[0]
    cap = slots // n
    part = rows // 2
    f32 = jnp.float32

    ocean = lax.ppermute(state, "sec", [(1, 0)])
    ocean = jnp.where(sec == 0, ocean, state)

    surface = state[:, levels - 1].reshape(3, rows // LANES, LANES)
    outgoing = pl.pallas_call(
        send_kernel,
        out_shape=jax.ShapeDtypeStruct((n, 3, cap // LANES, LANES), f32),
        in_specs=[VMEM] * 2,
        out_specs=VMEM,
        scratch_shapes=[pltpu.VMEM((3 * rows // LANES, 2 * LANES), jnp.bfloat16)],
        compiler_params=pltpu.CompilerParams(**PARAMS),
        name="pick_sent",
    )(surface, send_rows.reshape(-1, LANES))
    stepped = pl.pallas_call(
        functools.partial(advance_kernel, x_points, y_points),
        out_shape=jax.ShapeDtypeStruct(state.shape, f32),
        in_specs=[VMEM] * 3,
        out_specs=VMEM,
        compiler_params=pltpu.CompilerParams(**PARAMS),
        name="advance",
    )(state, atm_metric, jnp.broadcast_to(wave_speed[:, None], (levels, LANES)))
    rim = pl.pallas_call(
        edge_kernel,
        out_shape=jax.ShapeDtypeStruct((3, levels, 2 * y_points), f32),
        in_specs=[VMEM, SMEM],
        out_specs=VMEM,
        scratch_shapes=[pltpu.VMEM((rows, LANES), f32), pltpu.VMEM((2 * y_points, LANES), f32)],
        compiler_params=pltpu.CompilerParams(**PARAMS),
        name="pick_edges",
    )(ocean, ocean_edges.reshape(-1))

    border = jax.ShapeDtypeStruct((3, levels, y_points), f32)
    incoming, west_a, east_a, west_o, east_o = pl.pallas_call(
        functools.partial(exchange_kernel, n),
        out_shape=[jax.ShapeDtypeStruct(outgoing.shape, f32)] + [border] * 4,
        in_specs=[pl.BlockSpec(memory_space=pl.ANY)] * 3,
        out_specs=[pl.BlockSpec(memory_space=pl.ANY)] * 5,
        scratch_shapes=[pltpu.SemaphoreType.DMA((n,))] * 2 + [pltpu.SemaphoreType.DMA((4,))] * 2,
        compiler_params=pltpu.CompilerParams(collective_id=0, has_side_effects=True, **PARAMS),
        name="exchange",
    )(outgoing, stepped, rim)

    adjacent = lax.dynamic_slice_in_dim(ocean_adjacent, sec * part, part, 1).reshape(-1)
    kappa = lax.dynamic_slice_in_dim(ocean_kappa, sec * part, part, 0).reshape(1, -1)
    swept = pl.pallas_call(
        sweep_kernel,
        out_shape=jax.ShapeDtypeStruct((3, levels, part), f32),
        in_specs=[VMEM] * 3 + [SMEM, VMEM],
        out_specs=VMEM,
        scratch_shapes=[
            pltpu.VMEM((rows + 2 * y_points, LANES), f32),
            pltpu.VMEM((part, LANES), f32),
        ],
        compiler_params=pltpu.CompilerParams(**PARAMS),
        name="sweep",
    )(ocean, west_o, east_o, adjacent, kappa)
    helped = lax.ppermute(swept, "sec", [(0, 1)])

    regrid = pl.pallas_call(
        regrid_kernel,
        out_shape=jax.ShapeDtypeStruct((3, rows), f32),
        in_specs=[VMEM] * 3,
        out_specs=VMEM,
        scratch_shapes=[
            pltpu.VMEM((3 * slots // LANES, 2 * LANES), jnp.bfloat16),
            pltpu.VMEM((slots // LANES // 2, 2 * LANES), jnp.int32),
            pltpu.VMEM((slots // LANES // 2, 2 * LANES), f32),
        ],
        compiler_params=pltpu.CompilerParams(**PARAMS),
        cost_estimate=pl.CostEstimate(flops=6 * LANES * slots * slots // LANES, bytes_accessed=slots * 20, transcendentals=0),
        name="regrid",
    )(incoming, intersection_source.reshape(-1, LANES), intersection_weight.reshape(-1, LANES))

    return pl.pallas_call(
        functools.partial(finish_kernel, x_points, y_points),
        out_shape=jax.ShapeDtypeStruct(state.shape, f32),
        in_specs=[VMEM, SMEM] + [VMEM] * 5,
        out_specs=VMEM,
        compiler_params=pltpu.CompilerParams(**PARAMS),
        name="finish",
    )(regrid, couple_rate, stepped, west_a, east_a, swept, helped)


def solution(mesh):
    in_specs = (
        P(None, None, ("sec", "dom")),
        P(("sec", "dom")),
        P(("sec", "dom")),
        P(("sec", "dom")),
        P("sec", None),
        P(None, "dom"),
        P(),
        P(None, "dom"),
        P(None, "dom"),
        P("dom"),
    )
    out_specs = P(None, None, ("sec", "dom"))
    return jax.shard_map(body, mesh=mesh, in_specs=in_specs, out_specs=out_specs, check_vma=False)
```

```python
import functools
import jax
import jax.numpy as jnp
import numpy as np
from jax import lax
from jax.experimental import pallas as pl
from jax.experimental.pallas import tpu as pltpu
from jax.sharding import PartitionSpec as P

TIME_STEP = 0.05
LANES = 128
VMEM = pl.BlockSpec(memory_space=pltpu.VMEM)
SMEM = pl.BlockSpec(memory_space=pltpu.SMEM)
PARAMS = dict(vmem_limit_bytes=48 << 20)


def gll_derivative():
    nodes = np.array([-1.0, -1.0 / np.sqrt(5.0), 1.0 / np.sqrt(5.0), 1.0])
    barycentric = np.array(
        [1.0 / np.prod([nodes[i] - nodes[j] for j in range(4) if j != i]) for i in range(4)]
    )
    matrix = np.zeros((4, 4))
    for i in range(4):
        for j in range(4):
            if i != j:
                matrix[i, j] = barycentric[j] / barycentric[i] / (nodes[i] - nodes[j])
        matrix[i, i] = -np.sum(matrix[i])
    return matrix


DERIVATIVE = gll_derivative()


def two_terms(table):
    high = table.astype(jnp.bfloat16)
    low = (table - high.astype(jnp.float32)).astype(jnp.bfloat16)
    return jnp.concatenate([high, low], axis=1)


def pick(terms, depth, index):
    low = jnp.broadcast_to(index & (LANES - 1), (LANES, index.shape[1]))
    hot = (lax.broadcasted_iota(jnp.int32, low.shape, 0) == low).astype(jnp.float32).astype(jnp.bfloat16)
    found = jnp.dot(terms, jnp.concatenate([hot, hot], axis=0), preferred_element_type=jnp.float32)
    high = jnp.broadcast_to(index >> 7, (depth, index.shape[1]))
    own = lax.broadcasted_iota(jnp.int32, high.shape, 0) == high
    return [
        jnp.sum(jnp.where(own, found[f * depth : (f + 1) * depth], 0.0), axis=0, keepdims=True)
        for f in range(3)
    ]


def lane_phase(shape):
    return lax.broadcasted_iota(jnp.int32, shape, 1) % 4


def along_second(value, phase):
    width = value.shape[1]
    total = jnp.zeros_like(value)
    for shift in range(-3, 4):
        factor = jnp.zeros(value.shape, jnp.float32)
        for i in range(4):
            if 0 <= i + shift < 4:
                factor = jnp.where(phase == i, np.float32(DERIVATIVE[i, i + shift]), factor)
        moved = value if shift == 0 else pltpu.roll(value, (-shift) % width, 1)
        total = total + factor * moved
    return total


def advance(x_points, y_points, state_ref, metric_ref, speed_ref, stepped_ref):
    def piece(g, _):
        def at(i, f):
            return state_ref[f, :, pl.ds(pl.multiple_of(start + i * y_points, LANES), LANES)]

        start = (g // (y_points // LANES)) * 4 * y_points + (g % (y_points // LANES)) * LANES
        phase = lane_phase((state_ref.shape[1], LANES))
        u = [at(i, 0) for i in range(4)]
        v = [at(i, 1) for i in range(4)]
        h = [at(i, 2) for i in range(4)]
        speed = speed_ref[...]
        for i in range(4):
            here = pl.ds(pl.multiple_of(start + i * y_points, LANES), LANES)
            gx = metric_ref[0:1, here]
            gy = metric_ref[1:2, here]
            dx_h = sum(np.float32(DERIVATIVE[i, j]) * h[j] for j in range(4))
            dx_u = sum(np.float32(DERIVATIVE[i, j]) * u[j] for j in range(4))
            stepped_ref[0, :, here] = u[i] - TIME_STEP * (gx * dx_h)
            stepped_ref[1, :, here] = v[i] - TIME_STEP * (gy * along_second(h[i], phase))
            spread = gx * dx_u + gy * along_second(v[i], phase)
            stepped_ref[2, :, here] = h[i] - TIME_STEP * speed * spread
        return 0

    lax.fori_loop(0, x_points // 4 * (y_points // LANES), piece, 0)


def to_rows(source_ref, source_at, table_ref, table_at, count):
    def piece(c, _):
        here = pl.ds(pl.multiple_of(source_at + c * LANES, LANES), LANES)
        block = jnp.concatenate([source_ref[f, :, here] for f in range(3)], axis=0)
        there = pl.ds(pl.multiple_of(table_at + c * LANES, LANES), LANES)
        table_ref[there, : block.shape[0]] = jnp.transpose(block)
        return 0

    lax.fori_loop(0, count // LANES, piece, 0, unroll=4)


def from_rows(table_ref, at, levels):
    block = jnp.transpose(table_ref[pl.ds(pl.multiple_of(at, LANES), LANES), :])
    return [block[f * levels : (f + 1) * levels] for f in range(3)]


def pick_edges(state_ref, edges_ref, border_ref, table_ref, picked_ref):
    count = edges_ref.shape[0]
    to_rows(state_ref, 0, table_ref, 0, state_ref.shape[2])

    def step(i, _):
        base = i * 16
        places = [edges_ref[base + u] for u in range(16)]
        for u in range(16):
            picked_ref[pl.ds(base + u, 1), :] = table_ref[pl.ds(places[u], 1), :]
        return 0

    lax.fori_loop(0, count // 16, step, 0)
    for c in range(count // LANES):
        block = from_rows(picked_ref, c * LANES, state_ref.shape[1])
        for f in range(3):
            border_ref[f, :, c * LANES : (c + 1) * LANES] = block[f]


def prepare_kernel(
    n, x_points, y_points, surface_ref, rows_ref, state_ref, edges_ref, metric_ref, speed_ref,
    in_ref, stepped_ref, west_a_ref, east_a_ref, west_o_ref, east_o_ref,
    terms_ref, out_ref, rim_ref, table_ref, picked_ref, send_sem, recv_sem, edge_send_sem, edge_recv_sem,
):
    sec, dom = lax.axis_index("sec"), lax.axis_index("dom")
    right, left = lax.rem(dom + 1, n), lax.rem(dom + n - 1, n)
    mesh_ids = pl.DeviceIdType.MESH
    barrier = pltpu.get_barrier_semaphore()

    def greet(p, _):
        pl.semaphore_signal(barrier, inc=1, device_id=(1 - sec, p), device_id_type=mesh_ids)
        return 0

    lax.fori_loop(0, n, greet, 0)
    for side in (left, right):
        pl.semaphore_signal(barrier, inc=1, device_id=(sec, side), device_id_type=mesh_ids)

    @pl.when(sec == 0)
    def _():
        advance(x_points, y_points, state_ref, metric_ref, speed_ref, stepped_ref)

    @pl.when(sec == 1)
    def _():
        pick_edges(state_ref, edges_ref, rim_ref, table_ref, picked_ref)

    pl.semaphore_wait(barrier, n + 2)

    rows = state_ref.shape[2]
    first, last = pl.ds(0, y_points), pl.ds(rows - y_points, y_points)

    def edge(k, source, target, arrival, device):
        return pltpu.make_async_remote_copy(
            src_ref=source,
            dst_ref=target,
            send_sem=edge_send_sem.at[k],
            recv_sem=edge_recv_sem.at[arrival],
            device_id=device,
            device_id_type=mesh_ids,
        )

    rim_last, rim_first = rim_ref.at[:, :, pl.ds(y_points, y_points)], rim_ref.at[:, :, first]
    ocean_edges = [
        edge(0, rim_last, west_o_ref, 0, (1, right)),
        edge(1, rim_first, east_o_ref, 1, (1, left)),
        edge(2, rim_last, west_o_ref, 0, (0, right)),
        edge(3, rim_first, east_o_ref, 1, (0, left)),
    ]
    atmosphere_edges = [
        edge(0, stepped_ref.at[:, :, last], west_a_ref, 2, (0, right)),
        edge(1, stepped_ref.at[:, :, first], east_a_ref, 3, (0, left)),
    ]

    @pl.when(sec == 0)
    def _():
        for each in atmosphere_edges:
            each.start()

    @pl.when(sec == 1)
    def _():
        for each in ocean_edges:
            each.start()

    depth = surface_ref.shape[1]
    for f in range(3):
        terms_ref[f * depth : (f + 1) * depth, :] = two_terms(surface_ref[f])
    per_peer = out_ref.shape[2]

    def copy(k):
        p = lax.rem(dom + k, n)
        return pltpu.make_async_remote_copy(
            src_ref=out_ref.at[p],
            dst_ref=in_ref.at[dom],
            send_sem=send_sem.at[k],
            recv_sem=recv_sem.at[k],
            device_id=(1 - sec, p),
            device_id_type=mesh_ids,
        )

    def start(k, _):
        p = lax.rem(dom + k, n)
        for i in range(per_peer // 2):
            place = p * per_peer + 2 * i
            index = jnp.concatenate(
                [rows_ref[pl.ds(place, 1), :], rows_ref[pl.ds(place + 1, 1), :]], axis=1
            )
            values = pick(terms_ref[...], depth, index)
            for f in range(3):
                for half in range(2):
                    out_ref[p, f, 2 * i + half : 2 * i + half + 1, :] = values[f][
                        :, half * LANES : (half + 1) * LANES
                    ]
        copy(k).start()
        return 0

    def wait(k, _):
        copy(k).wait()
        return 0

    lax.fori_loop(0, n, start, 0)
    lax.fori_loop(0, n, wait, 0)

    @pl.when(sec == 0)
    def _():
        for each in atmosphere_edges:
            each.wait()
        ocean_edges[0].wait_recv()
        ocean_edges[1].wait_recv()

    @pl.when(sec == 1)
    def _():
        for each in ocean_edges:
            each.wait_send()
        ocean_edges[0].wait_recv()
        ocean_edges[1].wait_recv()


def sweep_kernel(state_ref, west_ref, east_ref, adjacent_ref, kappa_ref, swept_ref, table_ref, sum_ref):
    levels, rows, edge = state_ref.shape[1], state_ref.shape[2], west_ref.shape[2]
    part = swept_ref.shape[2]
    to_rows(state_ref, 0, table_ref, 0, rows)
    to_rows(west_ref, 0, table_ref, rows, edge)
    to_rows(east_ref, 0, table_ref, rows + edge, edge)

    def step(i, _):
        base = i * 16
        places = [[adjacent_ref[base + (j * part + u)] for j in range(6)] for u in range(16)]
        for u in range(16):
            a = [table_ref[pl.ds(p, 1), :] for p in places[u]]
            sum_ref[pl.ds(base + u, 1), :] = ((a[0] + a[1]) + (a[2] + a[3])) + (a[4] + a[5])
        return 0

    lax.fori_loop(0, part // 16, step, 0)
    first = lax.axis_index("sec") * part

    def finish(c, _):
        here = pl.ds(pl.multiple_of(c * LANES, LANES), LANES)
        there = pl.ds(pl.multiple_of(first + c * LANES, LANES), LANES)
        block = from_rows(sum_ref, c * LANES, levels)
        kappa = kappa_ref[0:1, here]
        for f in range(3):
            value = state_ref[f, :, there]
            swept_ref[f, :, here] = value + kappa * (block[f] - 6.0 * value)
        return 0

    lax.fori_loop(0, part // LANES, finish, 0, unroll=4)


def deinterleave(values, offset):
    count = values.shape[0]
    i = lax.broadcasted_iota(jnp.int32, (LANES, LANES), 0)
    j = lax.broadcasted_iota(jnp.int32, (LANES, LANES), 1)
    m = lax.broadcasted_iota(jnp.int32, (count // 2, count), 0)
    q = lax.broadcasted_iota(jnp.int32, (count // 2, count), 1)
    total = jnp.zeros((count // 2, LANES), jnp.float32)
    for b in range(2):
        chosen = (i == 2 * (j - b * (LANES // 2)) + offset).astype(jnp.float32)
        packed = jnp.dot(
            values, chosen, preferred_element_type=jnp.float32, precision=lax.Precision.HIGHEST
        )
        gathered = (q == 2 * m + b).astype(jnp.float32)
        total = total + jnp.dot(
            gathered, packed, preferred_element_type=jnp.float32, precision=lax.Precision.HIGHEST
        )
    return total


def regrid_kernel(incoming_ref, source_ref, weight_ref, regrid_ref, terms_ref, index_ref, share_ref):
    depth = source_ref.shape[0]
    for f in range(3):
        table = incoming_ref[:, f].reshape(depth, LANES)
        terms_ref[f * depth : (f + 1) * depth, :] = two_terms(table)
    source = source_ref[...].astype(jnp.float32)
    for k in range(2):
        index_ref[:, k * LANES : (k + 1) * LANES] = (deinterleave(source, k) + 0.5).astype(jnp.int32)
        share_ref[:, k * LANES : (k + 1) * LANES] = deinterleave(weight_ref[...], k)

    def step(c, _):
        values = pick(terms_ref[...], depth, index_ref[pl.ds(c, 1), :])
        weight = share_ref[pl.ds(c, 1), :]
        whole = weight[:, :LANES] + weight[:, LANES:]
        here = pl.ds(pl.multiple_of(c * LANES, LANES), LANES)
        for f in range(3):
            product = values[f] * weight
            regrid_ref[f : f + 1, here] = (product[:, :LANES] + product[:, LANES:]) / whole
        return 0

    lax.fori_loop(0, depth // 2, step, 0, unroll=4)


def finish_kernel(
    x_points, y_points, regrid_ref, rate_ref, stepped_ref, west_ref, east_ref, own_ref, helped_ref, new_ref,
):
    atmosphere = lax.axis_index("sec") == 0
    levels = stepped_ref.shape[1]

    def couple(f, here, value):
        rate = rate_ref[0, f]
        row = lax.broadcasted_iota(jnp.int32, value.shape, 0)
        relaxed = value + rate * (regrid_ref[f : f + 1, here] - value)
        new_ref[f, :, here] = jnp.where(row == levels - 1, relaxed, value)

    @pl.when(atmosphere)
    def _():
        for f in range(3):
            for x in range(x_points):
                here = slice(x * y_points, (x + 1) * y_points)
                value = stepped_ref[f, :, here]
                if x % 4 == 3:
                    other = (
                        stepped_ref[f, :, (x + 1) * y_points : (x + 2) * y_points]
                        if x < x_points - 1
                        else east_ref[f]
                    )
                    value = (value + other) * 0.5
                elif x % 4 == 0:
                    other = stepped_ref[f, :, (x - 1) * y_points : x * y_points] if x else west_ref[f]
                    value = (value + other) * 0.5
                position = lax.broadcasted_iota(jnp.int32, value.shape, 1)
                phase = position % 4
                after = pltpu.roll(value, y_points - 1, 1)
                before = pltpu.roll(value, 1, 1)
                averaged = jnp.where(
                    (phase == 3) & (position < y_points - 1),
                    (value + after) * 0.5,
                    jnp.where((phase == 0) & (position > 0), (value + before) * 0.5, value),
                )
                couple(f, here, averaged)

    @pl.when(jnp.logical_not(atmosphere))
    def _():
        part = own_ref.shape[2]
        for f in range(3):
            couple(f, slice(0, part), helped_ref[f])
            couple(f, slice(part, 2 * part), own_ref[f])


def body(
    state, send_rows, intersection_source, intersection_weight, couple_rate, atm_metric, wave_speed,
    ocean_adjacent, ocean_edges, ocean_kappa,
):
    levels, rows = state.shape[1], state.shape[2]
    y_points = ocean_edges.shape[1]
    x_points = rows // y_points
    n = lax.axis_size("dom")
    sec = lax.axis_index("sec")
    slots = send_rows.shape[0]
    cap = slots // n
    part = rows // 2
    f32 = jnp.float32

    ocean = lax.ppermute(state, "sec", [(1, 0)])
    ocean = jnp.where(sec == 0, ocean, state)

    surface = state[:, levels - 1].reshape(3, rows // LANES, LANES)
    border = jax.ShapeDtypeStruct((3, levels, y_points), f32)
    arriving = jax.ShapeDtypeStruct((n, 3, cap // LANES, LANES), f32)
    incoming, stepped, west_a, east_a, west_o, east_o = pl.pallas_call(
        functools.partial(prepare_kernel, n, x_points, y_points),
        out_shape=[arriving, jax.ShapeDtypeStruct(state.shape, f32)] + [border] * 4,
        in_specs=[VMEM] * 3 + [SMEM] + [VMEM] * 2,
        out_specs=[VMEM] * 6,
        scratch_shapes=[
            pltpu.VMEM((3 * rows // LANES, 2 * LANES), jnp.bfloat16),
            pltpu.VMEM(arriving.shape, f32),
            pltpu.VMEM((3, levels, 2 * y_points), f32),
            pltpu.VMEM((rows, LANES), f32),
            pltpu.VMEM((2 * y_points, LANES), f32),
            pltpu.SemaphoreType.DMA((n,)),
            pltpu.SemaphoreType.DMA((n,)),
            pltpu.SemaphoreType.DMA((4,)),
            pltpu.SemaphoreType.DMA((4,)),
        ],
        compiler_params=pltpu.CompilerParams(collective_id=0, has_side_effects=True, **PARAMS),
        cost_estimate=pl.CostEstimate(
            flops=6 * rows * LANES * slots // LANES, bytes_accessed=3 * state.size * 4, transcendentals=0
        ),
        name="prepare",
    )(
        surface,
        send_rows.reshape(-1, LANES),
        state,
        ocean_edges.reshape(-1),
        atm_metric,
        jnp.broadcast_to(wave_speed[:, None], (levels, LANES)),
    )

    adjacent = lax.dynamic_slice_in_dim(ocean_adjacent, sec * part, part, 1).reshape(-1)
    kappa = lax.dynamic_slice_in_dim(ocean_kappa, sec * part, part, 0).reshape(1, -1)
    swept = pl.pallas_call(
        sweep_kernel,
        out_shape=jax.ShapeDtypeStruct((3, levels, part), f32),
        in_specs=[VMEM] * 3 + [SMEM, VMEM],
        out_specs=VMEM,
        scratch_shapes=[
            pltpu.VMEM((rows + 2 * y_points, LANES), f32),
            pltpu.VMEM((part, LANES), f32),
        ],
        compiler_params=pltpu.CompilerParams(**PARAMS),
        name="sweep",
    )(ocean, west_o, east_o, adjacent, kappa)
    helped = lax.ppermute(swept, "sec", [(0, 1)])

    regrid = pl.pallas_call(
        regrid_kernel,
        out_shape=jax.ShapeDtypeStruct((3, rows), f32),
        in_specs=[VMEM] * 3,
        out_specs=VMEM,
        scratch_shapes=[
            pltpu.VMEM((3 * slots // LANES, 2 * LANES), jnp.bfloat16),
            pltpu.VMEM((slots // LANES // 2, 2 * LANES), jnp.int32),
            pltpu.VMEM((slots // LANES // 2, 2 * LANES), f32),
        ],
        compiler_params=pltpu.CompilerParams(**PARAMS),
        cost_estimate=pl.CostEstimate(flops=6 * LANES * slots * slots // LANES, bytes_accessed=slots * 20, transcendentals=0),
        name="regrid",
    )(incoming, intersection_source.reshape(-1, LANES), intersection_weight.reshape(-1, LANES))

    return pl.pallas_call(
        functools.partial(finish_kernel, x_points, y_points),
        out_shape=jax.ShapeDtypeStruct(state.shape, f32),
        in_specs=[VMEM, SMEM] + [VMEM] * 5,
        out_specs=VMEM,
        compiler_params=pltpu.CompilerParams(**PARAMS),
        name="finish",
    )(regrid, couple_rate, stepped, west_a, east_a, swept, helped)


def solution(mesh):
    in_specs = (
        P(None, None, ("sec", "dom")),
        P(("sec", "dom")),
        P(("sec", "dom")),
        P(("sec", "dom")),
        P("sec", None),
        P(None, "dom"),
        P(),
        P(None, "dom"),
        P(None, "dom"),
        P("dom"),
    )
    out_specs = P(None, None, ("sec", "dom"))
    return jax.shard_map(body, mesh=mesh, in_specs=in_specs, out_specs=out_specs, check_vma=False)
```

```python
import functools
import jax
import jax.numpy as jnp
import numpy as np
from jax import lax
from jax.experimental import pallas as pl
from jax.experimental.pallas import tpu as pltpu
from jax.sharding import PartitionSpec as P

TIME_STEP = 0.05
LANES = 128
VMEM = pl.BlockSpec(memory_space=pltpu.VMEM)
SMEM = pl.BlockSpec(memory_space=pltpu.SMEM)
PARAMS = dict(vmem_limit_bytes=48 << 20)


def gll_derivative():
    nodes = np.array([-1.0, -1.0 / np.sqrt(5.0), 1.0 / np.sqrt(5.0), 1.0])
    barycentric = np.array(
        [1.0 / np.prod([nodes[i] - nodes[j] for j in range(4) if j != i]) for i in range(4)]
    )
    matrix = np.zeros((4, 4))
    for i in range(4):
        for j in range(4):
            if i != j:
                matrix[i, j] = barycentric[j] / barycentric[i] / (nodes[i] - nodes[j])
        matrix[i, i] = -np.sum(matrix[i])
    return matrix


DERIVATIVE = gll_derivative()


def two_terms(table):
    high = table.astype(jnp.bfloat16)
    low = (table - high.astype(jnp.float32)).astype(jnp.bfloat16)
    return jnp.concatenate([high, low], axis=1)


def pick(terms, depth, index):
    low = jnp.broadcast_to(index & (LANES - 1), (LANES, index.shape[1]))
    hot = (lax.broadcasted_iota(jnp.int32, low.shape, 0) == low).astype(jnp.float32).astype(jnp.bfloat16)
    found = jnp.dot(terms, jnp.concatenate([hot, hot], axis=0), preferred_element_type=jnp.float32)
    high = jnp.broadcast_to(index >> 7, (depth, index.shape[1]))
    own = lax.broadcasted_iota(jnp.int32, high.shape, 0) == high
    return [
        jnp.sum(jnp.where(own, found[f * depth : (f + 1) * depth], 0.0), axis=0, keepdims=True)
        for f in range(3)
    ]


def lane_phase(shape):
    return lax.broadcasted_iota(jnp.int32, shape, 1) % 4


def along_second(value, phase):
    width = value.shape[1]
    total = jnp.zeros_like(value)
    for shift in range(-3, 4):
        factor = jnp.zeros(value.shape, jnp.float32)
        for i in range(4):
            if 0 <= i + shift < 4:
                factor = jnp.where(phase == i, np.float32(DERIVATIVE[i, i + shift]), factor)
        moved = value if shift == 0 else pltpu.roll(value, (-shift) % width, 1)
        total = total + factor * moved
    return total


def advance(x_points, y_points, state_ref, metric_ref, speed_ref, stepped_ref):
    level = lax.broadcasted_iota(jnp.int32, (state_ref.shape[1], LANES), 0)
    speed = jnp.zeros(level.shape, jnp.float32)
    for k in range(level.shape[0]):
        speed = jnp.where(level == k, speed_ref[k], speed)

    def piece(g, _):
        def at(i, f):
            return state_ref[f, :, pl.ds(pl.multiple_of(start + i * y_points, LANES), LANES)]

        start = (g // (y_points // LANES)) * 4 * y_points + (g % (y_points // LANES)) * LANES
        phase = lane_phase((state_ref.shape[1], LANES))
        u = [at(i, 0) for i in range(4)]
        v = [at(i, 1) for i in range(4)]
        h = [at(i, 2) for i in range(4)]
        for i in range(4):
            here = pl.ds(pl.multiple_of(start + i * y_points, LANES), LANES)
            gx = metric_ref[0:1, here]
            gy = metric_ref[1:2, here]
            dx_h = sum(np.float32(DERIVATIVE[i, j]) * h[j] for j in range(4))
            dx_u = sum(np.float32(DERIVATIVE[i, j]) * u[j] for j in range(4))
            stepped_ref[0, :, here] = u[i] - TIME_STEP * (gx * dx_h)
            stepped_ref[1, :, here] = v[i] - TIME_STEP * (gy * along_second(h[i], phase))
            spread = gx * dx_u + gy * along_second(v[i], phase)
            stepped_ref[2, :, here] = h[i] - TIME_STEP * speed * spread
        return 0

    lax.fori_loop(0, x_points // 4 * (y_points // LANES), piece, 0)


def to_rows(source_ref, source_at, table_ref, table_at, count):
    def piece(c, _):
        here = pl.ds(pl.multiple_of(source_at + c * LANES, LANES), LANES)
        block = jnp.concatenate([source_ref[f, :, here] for f in range(3)], axis=0)
        there = pl.ds(pl.multiple_of(table_at + c * LANES, LANES), LANES)
        table_ref[there, : block.shape[0]] = jnp.transpose(block)
        return 0

    lax.fori_loop(0, count // LANES, piece, 0, unroll=4)


def from_rows(table_ref, at, levels):
    block = jnp.transpose(table_ref[pl.ds(pl.multiple_of(at, LANES), LANES), :])
    return [block[f * levels : (f + 1) * levels] for f in range(3)]


def pick_edges(state_ref, edges_ref, border_ref, table_ref, picked_ref):
    side = edges_ref.shape[1]
    count = 2 * side
    to_rows(state_ref, 0, table_ref, 0, state_ref.shape[2])

    def step(i, _):
        base = i * 8
        places = [[edges_ref[k, base + u] for u in range(8)] for k in range(2)]
        for k in range(2):
            for u in range(8):
                picked_ref[pl.ds(k * side + base + u, 1), :] = table_ref[pl.ds(places[k][u], 1), :]
        return 0

    lax.fori_loop(0, side // 8, step, 0)
    for c in range(count // LANES):
        block = from_rows(picked_ref, c * LANES, state_ref.shape[1])
        for f in range(3):
            border_ref[f, :, c * LANES : (c + 1) * LANES] = block[f]


def prepare_kernel(
    n, x_points, y_points, rows_ref, state_ref, edges_ref, metric_ref, speed_ref,
    in_ref, stepped_ref, west_a_ref, east_a_ref, west_o_ref, east_o_ref,
    surface_ref, terms_ref, out_ref, rim_ref, table_ref, picked_ref, send_sem, recv_sem, edge_send_sem, edge_recv_sem,
):
    sec, dom = lax.axis_index("sec"), lax.axis_index("dom")
    right, left = lax.rem(dom + 1, n), lax.rem(dom + n - 1, n)
    mesh_ids = pl.DeviceIdType.MESH
    barrier = pltpu.get_barrier_semaphore()

    def greet(p, _):
        pl.semaphore_signal(barrier, inc=1, device_id=(1 - sec, p), device_id_type=mesh_ids)
        return 0

    lax.fori_loop(0, n, greet, 0)
    for side in (left, right):
        pl.semaphore_signal(barrier, inc=1, device_id=(sec, side), device_id_type=mesh_ids)

    @pl.when(sec == 0)
    def _():
        advance(x_points, y_points, state_ref, metric_ref, speed_ref, stepped_ref)

    @pl.when(sec == 1)
    def _():
        pick_edges(state_ref, edges_ref, rim_ref, table_ref, picked_ref)

    pl.semaphore_wait(barrier, n + 2)

    rows = state_ref.shape[2]
    first, last = pl.ds(0, y_points), pl.ds(rows - y_points, y_points)

    def edge(k, source, target, arrival, device):
        return pltpu.make_async_remote_copy(
            src_ref=source,
            dst_ref=target,
            send_sem=edge_send_sem.at[k],
            recv_sem=edge_recv_sem.at[arrival],
            device_id=device,
            device_id_type=mesh_ids,
        )

    rim_last, rim_first = rim_ref.at[:, :, pl.ds(y_points, y_points)], rim_ref.at[:, :, first]
    ocean_edges = [
        edge(0, rim_last, west_o_ref, 0, (1, right)),
        edge(1, rim_first, east_o_ref, 1, (1, left)),
        edge(2, rim_last, west_o_ref, 0, (0, right)),
        edge(3, rim_first, east_o_ref, 1, (0, left)),
    ]
    atmosphere_edges = [
        edge(0, stepped_ref.at[:, :, last], west_a_ref, 2, (0, right)),
        edge(1, stepped_ref.at[:, :, first], east_a_ref, 3, (0, left)),
    ]

    @pl.when(sec == 0)
    def _():
        for each in atmosphere_edges:
            each.start()

    @pl.when(sec == 1)
    def _():
        for each in ocean_edges:
            each.start()

    depth, top = rows // LANES, state_ref.shape[1] - 1
    for h in range(depth):
        for f in range(3):
            surface_ref[f * depth + h : f * depth + h + 1, :] = state_ref[
                f, top : top + 1, h * LANES : (h + 1) * LANES
            ]
    terms_ref[...] = two_terms(surface_ref[...])
    per_peer = out_ref.shape[2]

    def copy(k):
        p = lax.rem(dom + k, n)
        return pltpu.make_async_remote_copy(
            src_ref=out_ref.at[p],
            dst_ref=in_ref.at[dom],
            send_sem=send_sem.at[k],
            recv_sem=recv_sem.at[k],
            device_id=(1 - sec, p),
            device_id_type=mesh_ids,
        )

    def start(k, _):
        p = lax.rem(dom + k, n)
        for i in range(per_peer // 2):
            place = p * per_peer + 2 * i
            index = jnp.concatenate(
                [rows_ref[pl.ds(place, 1), :], rows_ref[pl.ds(place + 1, 1), :]], axis=1
            )
            values = pick(terms_ref[...], depth, index)
            for f in range(3):
                for half in range(2):
                    out_ref[p, f, 2 * i + half : 2 * i + half + 1, :] = values[f][
                        :, half * LANES : (half + 1) * LANES
                    ]
        copy(k).start()
        return 0

    def wait(k, _):
        copy(k).wait()
        return 0

    lax.fori_loop(0, n, start, 0)
    lax.fori_loop(0, n, wait, 0)

    @pl.when(sec == 0)
    def _():
        for each in atmosphere_edges:
            each.wait()
        ocean_edges[0].wait_recv()
        ocean_edges[1].wait_recv()

    @pl.when(sec == 1)
    def _():
        for each in ocean_edges:
            each.wait_send()
        ocean_edges[0].wait_recv()
        ocean_edges[1].wait_recv()


def deinterleave(values, offset):
    count = values.shape[0]
    i = lax.broadcasted_iota(jnp.int32, (LANES, LANES), 0)
    j = lax.broadcasted_iota(jnp.int32, (LANES, LANES), 1)
    m = lax.broadcasted_iota(jnp.int32, (count // 2, count), 0)
    q = lax.broadcasted_iota(jnp.int32, (count // 2, count), 1)
    total = jnp.zeros((count // 2, LANES), jnp.float32)
    for b in range(2):
        chosen = (i == 2 * (j - b * (LANES // 2)) + offset).astype(jnp.float32)
        packed = jnp.dot(
            values, chosen, preferred_element_type=jnp.float32, precision=lax.Precision.HIGHEST
        )
        gathered = (q == 2 * m + b).astype(jnp.float32)
        total = total + jnp.dot(
            gathered, packed, preferred_element_type=jnp.float32, precision=lax.Precision.HIGHEST
        )
    return total


def sweep_kernel(
    state_ref, west_ref, east_ref, adjacent_ref, kappa_ref, incoming_ref, source_ref, weight_ref,
    swept_ref, regrid_ref, table_ref, sum_ref, terms_ref, index_ref, share_ref,
):
    levels, rows, edge = state_ref.shape[1], state_ref.shape[2], west_ref.shape[2]
    part = swept_ref.shape[2]
    to_rows(state_ref, 0, table_ref, 0, rows)
    to_rows(west_ref, 0, table_ref, rows, edge)
    to_rows(east_ref, 0, table_ref, rows + edge, edge)

    depth = source_ref.shape[0]
    for f in range(3):
        table = incoming_ref[:, f].reshape(depth, LANES)
        terms_ref[f * depth : (f + 1) * depth, :] = two_terms(table)
    source = source_ref[...].astype(jnp.float32)
    for k in range(2):
        index_ref[:, k * LANES : (k + 1) * LANES] = (deinterleave(source, k) + 0.5).astype(jnp.int32)
        share_ref[:, k * LANES : (k + 1) * LANES] = deinterleave(weight_ref[...], k)

    steps = depth // 2
    cells = part // steps

    def step(c, _):
        values = pick(terms_ref[...], depth, index_ref[pl.ds(c, 1), :])
        for u in range(cells):
            cell = c * cells + u
            places = [adjacent_ref[c * cells + (j * part + u)] for j in range(6)]
            a = [table_ref[pl.ds(p, 1), :] for p in places]
            sum_ref[pl.ds(cell, 1), :] = ((a[0] + a[1]) + (a[2] + a[3])) + (a[4] + a[5])
        weight = share_ref[pl.ds(c, 1), :]
        whole = weight[:, :LANES] + weight[:, LANES:]
        here = pl.ds(pl.multiple_of(c * LANES, LANES), LANES)
        for f in range(3):
            product = values[f] * weight
            regrid_ref[f : f + 1, here] = (product[:, :LANES] + product[:, LANES:]) / whole
        return 0

    lax.fori_loop(0, steps, step, 0)
    first = lax.axis_index("sec") * (part // LANES)

    def finish(c, _):
        here = pl.ds(pl.multiple_of(c * LANES, LANES), LANES)
        there = pl.ds(pl.multiple_of((first + c) * LANES, LANES), LANES)
        block = from_rows(sum_ref, c * LANES, levels)
        kappa = kappa_ref[pl.ds(first + c, 1), :]
        for f in range(3):
            value = state_ref[f, :, there]
            swept_ref[f, :, here] = value + kappa * (block[f] - 6.0 * value)
        return 0

    lax.fori_loop(0, part // LANES, finish, 0, unroll=4)


def finish_kernel(
    x_points, y_points, regrid_ref, rate_ref, stepped_ref, west_ref, east_ref, own_ref, helped_ref, new_ref,
):
    atmosphere = lax.axis_index("sec") == 0
    levels = stepped_ref.shape[1]

    def couple(f, here, value):
        rate = rate_ref[0, f]
        row = lax.broadcasted_iota(jnp.int32, value.shape, 0)
        relaxed = value + rate * (regrid_ref[f : f + 1, here] - value)
        new_ref[f, :, here] = jnp.where(row == levels - 1, relaxed, value)

    @pl.when(atmosphere)
    def _():
        for f in range(3):
            for x in range(x_points):
                here = slice(x * y_points, (x + 1) * y_points)
                value = stepped_ref[f, :, here]
                if x % 4 == 3:
                    other = (
                        stepped_ref[f, :, (x + 1) * y_points : (x + 2) * y_points]
                        if x < x_points - 1
                        else east_ref[f]
                    )
                    value = (value + other) * 0.5
                elif x % 4 == 0:
                    other = stepped_ref[f, :, (x - 1) * y_points : x * y_points] if x else west_ref[f]
                    value = (value + other) * 0.5
                position = lax.broadcasted_iota(jnp.int32, value.shape, 1)
                phase = position % 4
                after = pltpu.roll(value, y_points - 1, 1)
                before = pltpu.roll(value, 1, 1)
                averaged = jnp.where(
                    (phase == 3) & (position < y_points - 1),
                    (value + after) * 0.5,
                    jnp.where((phase == 0) & (position > 0), (value + before) * 0.5, value),
                )
                couple(f, here, averaged)

    @pl.when(jnp.logical_not(atmosphere))
    def _():
        part = own_ref.shape[2]
        for f in range(3):
            couple(f, slice(0, part), helped_ref[f])
            couple(f, slice(part, 2 * part), own_ref[f])


def body(
    state, send_rows, intersection_source, intersection_weight, couple_rate, atm_metric, wave_speed,
    ocean_adjacent, ocean_edges, ocean_kappa,
):
    levels, rows = state.shape[1], state.shape[2]
    y_points = ocean_edges.shape[1]
    x_points = rows // y_points
    n = lax.axis_size("dom")
    sec = lax.axis_index("sec")
    slots = send_rows.shape[0]
    cap = slots // n
    part = rows // 2
    f32 = jnp.float32

    ocean = lax.ppermute(state, "sec", [(1, 0)])
    ocean = jnp.where(sec == 0, ocean, state)

    border = jax.ShapeDtypeStruct((3, levels, y_points), f32)
    arriving = jax.ShapeDtypeStruct((n, 3, cap // LANES, LANES), f32)
    incoming, stepped, west_a, east_a, west_o, east_o = pl.pallas_call(
        functools.partial(prepare_kernel, n, x_points, y_points),
        out_shape=[arriving, jax.ShapeDtypeStruct(state.shape, f32)] + [border] * 4,
        in_specs=[VMEM] * 2 + [SMEM, VMEM, SMEM],
        out_specs=[VMEM] * 6,
        scratch_shapes=[
            pltpu.VMEM((3 * rows // LANES, LANES), f32),
            pltpu.VMEM((3 * rows // LANES, 2 * LANES), jnp.bfloat16),
            pltpu.VMEM(arriving.shape, f32),
            pltpu.VMEM((3, levels, 2 * y_points), f32),
            pltpu.VMEM((rows, LANES), f32),
            pltpu.VMEM((2 * y_points, LANES), f32),
            pltpu.SemaphoreType.DMA((n,)),
            pltpu.SemaphoreType.DMA((n,)),
            pltpu.SemaphoreType.DMA((4,)),
            pltpu.SemaphoreType.DMA((4,)),
        ],
        compiler_params=pltpu.CompilerParams(collective_id=0, has_side_effects=True, **PARAMS),
        cost_estimate=pl.CostEstimate(
            flops=6 * rows * LANES * slots // LANES, bytes_accessed=3 * state.size * 4, transcendentals=0
        ),
        name="prepare",
    )(
        send_rows.reshape(-1, LANES),
        state,
        ocean_edges,
        atm_metric,
        wave_speed,
    )

    adjacent = lax.dynamic_slice_in_dim(ocean_adjacent, sec * part, part, 1).reshape(-1)
    swept, regrid = pl.pallas_call(
        sweep_kernel,
        out_shape=[jax.ShapeDtypeStruct((3, levels, part), f32), jax.ShapeDtypeStruct((3, rows), f32)],
        in_specs=[VMEM] * 3 + [SMEM] + [VMEM] * 4,
        out_specs=[VMEM] * 2,
        scratch_shapes=[
            pltpu.VMEM((rows + 2 * y_points, LANES), f32),
            pltpu.VMEM((part, LANES), f32),
            pltpu.VMEM((3 * slots // LANES, 2 * LANES), jnp.bfloat16),
            pltpu.VMEM((slots // LANES // 2, 2 * LANES), jnp.int32),
            pltpu.VMEM((slots // LANES // 2, 2 * LANES), f32),
        ],
        compiler_params=pltpu.CompilerParams(**PARAMS),
        name="sweep",
    )(
        ocean, west_o, east_o, adjacent, ocean_kappa.reshape(-1, LANES), incoming,
        intersection_source.reshape(-1, LANES), intersection_weight.reshape(-1, LANES),
    )
    helped = lax.ppermute(swept, "sec", [(0, 1)])

    return pl.pallas_call(
        functools.partial(finish_kernel, x_points, y_points),
        out_shape=jax.ShapeDtypeStruct(state.shape, f32),
        in_specs=[VMEM, SMEM] + [VMEM] * 5,
        out_specs=VMEM,
        compiler_params=pltpu.CompilerParams(**PARAMS),
        name="finish",
    )(regrid, couple_rate, stepped, west_a, east_a, swept, helped)


def solution(mesh):
    in_specs = (
        P(None, None, ("sec", "dom")),
        P(("sec", "dom")),
        P(("sec", "dom")),
        P(("sec", "dom")),
        P("sec", None),
        P(None, "dom"),
        P(),
        P(None, "dom"),
        P(None, "dom"),
        P("dom"),
    )
    out_specs = P(None, None, ("sec", "dom"))
    return jax.shard_map(body, mesh=mesh, in_specs=in_specs, out_specs=out_specs, check_vma=False)
```

```python
import functools
import jax
import jax.numpy as jnp
import numpy as np
from jax import lax
from jax.experimental import pallas as pl
from jax.experimental.pallas import tpu as pltpu
from jax.sharding import PartitionSpec as P

TIME_STEP = 0.05
LANES = 128
VMEM = pl.BlockSpec(memory_space=pltpu.VMEM)
SMEM = pl.BlockSpec(memory_space=pltpu.SMEM)
PARAMS = dict(vmem_limit_bytes=48 << 20)


def gll_derivative():
    nodes = np.array([-1.0, -1.0 / np.sqrt(5.0), 1.0 / np.sqrt(5.0), 1.0])
    barycentric = np.array(
        [1.0 / np.prod([nodes[i] - nodes[j] for j in range(4) if j != i]) for i in range(4)]
    )
    matrix = np.zeros((4, 4))
    for i in range(4):
        for j in range(4):
            if i != j:
                matrix[i, j] = barycentric[j] / barycentric[i] / (nodes[i] - nodes[j])
        matrix[i, i] = -np.sum(matrix[i])
    return matrix


DERIVATIVE = gll_derivative()


def two_terms(table):
    high = table.astype(jnp.bfloat16)
    low = (table - high.astype(jnp.float32)).astype(jnp.bfloat16)
    return jnp.concatenate([high, low], axis=1)


def pick(terms, depth, index):
    low = jnp.broadcast_to(index & (LANES - 1), (LANES, index.shape[1]))
    hot = (lax.broadcasted_iota(jnp.int32, low.shape, 0) == low).astype(jnp.float32).astype(jnp.bfloat16)
    found = jnp.dot(terms, jnp.concatenate([hot, hot], axis=0), preferred_element_type=jnp.float32)
    high = jnp.broadcast_to(index >> 7, (depth, index.shape[1]))
    own = lax.broadcasted_iota(jnp.int32, high.shape, 0) == high
    return [
        jnp.sum(jnp.where(own, found[f * depth : (f + 1) * depth], 0.0), axis=0, keepdims=True)
        for f in range(3)
    ]


def lane_phase(shape):
    return lax.broadcasted_iota(jnp.int32, shape, 1) % 4


def along_second(value, phase):
    width = value.shape[1]
    total = jnp.zeros_like(value)
    for shift in range(-3, 4):
        factor = jnp.zeros(value.shape, jnp.float32)
        for i in range(4):
            if 0 <= i + shift < 4:
                factor = jnp.where(phase == i, np.float32(DERIVATIVE[i, i + shift]), factor)
        moved = value if shift == 0 else pltpu.roll(value, (-shift) % width, 1)
        total = total + factor * moved
    return total


def advance(x_points, y_points, state_ref, metric_ref, speed_ref, stepped_ref):
    level = lax.broadcasted_iota(jnp.int32, (state_ref.shape[1], LANES), 0)
    speed = jnp.zeros(level.shape, jnp.float32)
    for k in range(level.shape[0]):
        speed = jnp.where(level == k, speed_ref[k], speed)

    def piece(g, _):
        def at(i, f):
            return state_ref[f, :, pl.ds(pl.multiple_of(start + i * y_points, LANES), LANES)]

        start = (g // (y_points // LANES)) * 4 * y_points + (g % (y_points // LANES)) * LANES
        phase = lane_phase((state_ref.shape[1], LANES))
        u = [at(i, 0) for i in range(4)]
        v = [at(i, 1) for i in range(4)]
        h = [at(i, 2) for i in range(4)]
        for i in range(4):
            here = pl.ds(pl.multiple_of(start + i * y_points, LANES), LANES)
            gx = metric_ref[0:1, here]
            gy = metric_ref[1:2, here]
            dx_h = sum(np.float32(DERIVATIVE[i, j]) * h[j] for j in range(4))
            dx_u = sum(np.float32(DERIVATIVE[i, j]) * u[j] for j in range(4))
            stepped_ref[0, :, here] = u[i] - TIME_STEP * (gx * dx_h)
            stepped_ref[1, :, here] = v[i] - TIME_STEP * (gy * along_second(h[i], phase))
            spread = gx * dx_u + gy * along_second(v[i], phase)
            stepped_ref[2, :, here] = h[i] - TIME_STEP * speed * spread
        return 0

    lax.fori_loop(0, x_points // 4 * (y_points // LANES), piece, 0)


def to_rows(source_ref, source_at, table_ref, table_at, count):
    def piece(c, _):
        here = pl.ds(pl.multiple_of(source_at + c * LANES, LANES), LANES)
        block = jnp.concatenate([source_ref[f, :, here] for f in range(3)], axis=0)
        there = pl.ds(pl.multiple_of(table_at + c * LANES, LANES), LANES)
        table_ref[there, : block.shape[0]] = jnp.transpose(block)
        return 0

    lax.fori_loop(0, count // LANES, piece, 0, unroll=4)


def from_rows(table_ref, at, levels):
    block = jnp.transpose(table_ref[pl.ds(pl.multiple_of(at, LANES), LANES), :])
    return [block[f * levels : (f + 1) * levels] for f in range(3)]


def pick_edges(state_ref, edges_ref, border_ref, table_ref, picked_ref):
    side = edges_ref.shape[1]
    count = 2 * side
    to_rows(state_ref, 0, table_ref, 0, state_ref.shape[2])

    def step(i, _):
        base = i * 8
        places = [[edges_ref[k, base + u] for u in range(8)] for k in range(2)]
        for k in range(2):
            for u in range(8):
                picked_ref[pl.ds(k * side + base + u, 1), :] = table_ref[pl.ds(places[k][u], 1), :]
        return 0

    lax.fori_loop(0, side // 8, step, 0)
    for c in range(count // LANES):
        block = from_rows(picked_ref, c * LANES, state_ref.shape[1])
        for f in range(3):
            border_ref[f, :, c * LANES : (c + 1) * LANES] = block[f]


def prepare_kernel(
    n, x_points, y_points, rows_ref, state_ref, edges_ref, metric_ref, speed_ref,
    in_ref, stepped_ref, west_a_ref, east_a_ref, west_o_ref, east_o_ref, ocean_ref,
    surface_ref, terms_ref, out_ref, rim_ref, table_ref, picked_ref, send_sem, recv_sem, edge_send_sem, edge_recv_sem,
):
    sec, dom = lax.axis_index("sec"), lax.axis_index("dom")
    right, left = lax.rem(dom + 1, n), lax.rem(dom + n - 1, n)
    mesh_ids = pl.DeviceIdType.MESH
    barrier = pltpu.get_barrier_semaphore()

    def greet(p, _):
        pl.semaphore_signal(barrier, inc=1, device_id=(1 - sec, p), device_id_type=mesh_ids)
        return 0

    lax.fori_loop(0, n, greet, 0)
    for side in (left, right):
        pl.semaphore_signal(barrier, inc=1, device_id=(sec, side), device_id_type=mesh_ids)

    @pl.when(sec == 0)
    def _():
        advance(x_points, y_points, state_ref, metric_ref, speed_ref, stepped_ref)

    @pl.when(sec == 1)
    def _():
        pick_edges(state_ref, edges_ref, rim_ref, table_ref, picked_ref)

    pl.semaphore_wait(barrier, n + 2)

    rows = state_ref.shape[2]
    first, last = pl.ds(0, y_points), pl.ds(rows - y_points, y_points)

    def edge(k, source, target, arrival, device):
        return pltpu.make_async_remote_copy(
            src_ref=source,
            dst_ref=target,
            send_sem=edge_send_sem.at[k],
            recv_sem=edge_recv_sem.at[arrival],
            device_id=device,
            device_id_type=mesh_ids,
        )

    rim_last, rim_first = rim_ref.at[:, :, pl.ds(y_points, y_points)], rim_ref.at[:, :, first]
    ocean_edges = [
        edge(0, rim_last, west_o_ref, 0, (1, right)),
        edge(1, rim_first, east_o_ref, 1, (1, left)),
        edge(2, rim_last, west_o_ref, 0, (0, right)),
        edge(3, rim_first, east_o_ref, 1, (0, left)),
        edge(4, state_ref, ocean_ref, 4, (0, dom)),
    ]
    atmosphere_edges = [
        edge(0, stepped_ref.at[:, :, last], west_a_ref, 2, (0, right)),
        edge(1, stepped_ref.at[:, :, first], east_a_ref, 3, (0, left)),
    ]

    @pl.when(sec == 0)
    def _():
        for each in atmosphere_edges:
            each.start()

    @pl.when(sec == 1)
    def _():
        for each in ocean_edges:
            each.start()

    depth, top = rows // LANES, state_ref.shape[1] - 1
    for h in range(depth):
        for f in range(3):
            surface_ref[f * depth + h : f * depth + h + 1, :] = state_ref[
                f, top : top + 1, h * LANES : (h + 1) * LANES
            ]
    terms_ref[...] = two_terms(surface_ref[...])
    per_peer = out_ref.shape[2]

    def copy(k):
        p = lax.rem(dom + k, n)
        return pltpu.make_async_remote_copy(
            src_ref=out_ref.at[p],
            dst_ref=in_ref.at[dom],
            send_sem=send_sem.at[k],
            recv_sem=recv_sem.at[k],
            device_id=(1 - sec, p),
            device_id_type=mesh_ids,
        )

    def start(k, _):
        p = lax.rem(dom + k, n)
        for i in range(per_peer // 2):
            place = p * per_peer + 2 * i
            index = jnp.concatenate(
                [rows_ref[pl.ds(place, 1), :], rows_ref[pl.ds(place + 1, 1), :]], axis=1
            )
            values = pick(terms_ref[...], depth, index)
            for f in range(3):
                for half in range(2):
                    out_ref[p, f, 2 * i + half : 2 * i + half + 1, :] = values[f][
                        :, half * LANES : (half + 1) * LANES
                    ]
        copy(k).start()
        return 0

    def wait(k, _):
        copy(k).wait()
        return 0

    lax.fori_loop(0, n, start, 0)
    lax.fori_loop(0, n, wait, 0)

    @pl.when(sec == 0)
    def _():
        for each in atmosphere_edges:
            each.wait()
        ocean_edges[0].wait_recv()
        ocean_edges[1].wait_recv()
        ocean_edges[4].wait_recv()

    @pl.when(sec == 1)
    def _():
        for each in ocean_edges:
            each.wait_send()
        ocean_edges[0].wait_recv()
        ocean_edges[1].wait_recv()


def deinterleave(values, offset):
    count = values.shape[0]
    i = lax.broadcasted_iota(jnp.int32, (LANES, LANES), 0)
    j = lax.broadcasted_iota(jnp.int32, (LANES, LANES), 1)
    m = lax.broadcasted_iota(jnp.int32, (count // 2, count), 0)
    q = lax.broadcasted_iota(jnp.int32, (count // 2, count), 1)
    total = jnp.zeros((count // 2, LANES), jnp.float32)
    for b in range(2):
        chosen = (i == 2 * (j - b * (LANES // 2)) + offset).astype(jnp.float32)
        packed = jnp.dot(
            values, chosen, preferred_element_type=jnp.float32, precision=lax.Precision.HIGHEST
        )
        gathered = (q == 2 * m + b).astype(jnp.float32)
        total = total + jnp.dot(
            gathered, packed, preferred_element_type=jnp.float32, precision=lax.Precision.HIGHEST
        )
    return total


def sweep_kernel(
    state_ref, west_ref, east_ref, adjacent_ref, kappa_ref, incoming_ref, source_ref, weight_ref,
    swept_ref, regrid_ref, table_ref, sum_ref, terms_ref, index_ref, share_ref,
):
    levels, rows, edge = state_ref.shape[1], state_ref.shape[2], west_ref.shape[2]
    part = swept_ref.shape[2]
    to_rows(state_ref, 0, table_ref, 0, rows)
    to_rows(west_ref, 0, table_ref, rows, edge)
    to_rows(east_ref, 0, table_ref, rows + edge, edge)

    depth = source_ref.shape[0]
    for f in range(3):
        table = incoming_ref[:, f].reshape(depth, LANES)
        terms_ref[f * depth : (f + 1) * depth, :] = two_terms(table)
    source = source_ref[...].astype(jnp.float32)
    for k in range(2):
        index_ref[:, k * LANES : (k + 1) * LANES] = (deinterleave(source, k) + 0.5).astype(jnp.int32)
        share_ref[:, k * LANES : (k + 1) * LANES] = deinterleave(weight_ref[...], k)

    steps = depth // 2
    cells = part // steps

    def step(c, _):
        values = pick(terms_ref[...], depth, index_ref[pl.ds(c, 1), :])
        for u in range(cells):
            cell = c * cells + u
            places = [adjacent_ref[c * cells + (j * part + u)] for j in range(6)]
            a = [table_ref[pl.ds(p, 1), :] for p in places]
            sum_ref[pl.ds(cell, 1), :] = ((a[0] + a[1]) + (a[2] + a[3])) + (a[4] + a[5])
        weight = share_ref[pl.ds(c, 1), :]
        whole = weight[:, :LANES] + weight[:, LANES:]
        here = pl.ds(pl.multiple_of(c * LANES, LANES), LANES)
        for f in range(3):
            product = values[f] * weight
            regrid_ref[f : f + 1, here] = (product[:, :LANES] + product[:, LANES:]) / whole
        return 0

    lax.fori_loop(0, steps, step, 0)
    first = lax.axis_index("sec") * (part // LANES)

    def finish(c, _):
        here = pl.ds(pl.multiple_of(c * LANES, LANES), LANES)
        there = pl.ds(pl.multiple_of((first + c) * LANES, LANES), LANES)
        block = from_rows(sum_ref, c * LANES, levels)
        kappa = kappa_ref[pl.ds(first + c, 1), :]
        for f in range(3):
            value = state_ref[f, :, there]
            swept_ref[f, :, here] = value + kappa * (block[f] - 6.0 * value)
        return 0

    lax.fori_loop(0, part // LANES, finish, 0, unroll=4)


def finish_kernel(
    x_points, y_points, regrid_ref, rate_ref, stepped_ref, west_ref, east_ref, own_ref, helped_ref, new_ref,
):
    atmosphere = lax.axis_index("sec") == 0
    levels = stepped_ref.shape[1]

    def couple(f, here, value):
        rate = rate_ref[0, f]
        row = lax.broadcasted_iota(jnp.int32, value.shape, 0)
        relaxed = value + rate * (regrid_ref[f : f + 1, here] - value)
        new_ref[f, :, here] = jnp.where(row == levels - 1, relaxed, value)

    @pl.when(atmosphere)
    def _():
        for f in range(3):
            for x in range(x_points):
                here = slice(x * y_points, (x + 1) * y_points)
                value = stepped_ref[f, :, here]
                if x % 4 == 3:
                    other = (
                        stepped_ref[f, :, (x + 1) * y_points : (x + 2) * y_points]
                        if x < x_points - 1
                        else east_ref[f]
                    )
                    value = (value + other) * 0.5
                elif x % 4 == 0:
                    other = stepped_ref[f, :, (x - 1) * y_points : x * y_points] if x else west_ref[f]
                    value = (value + other) * 0.5
                position = lax.broadcasted_iota(jnp.int32, value.shape, 1)
                phase = position % 4
                after = pltpu.roll(value, y_points - 1, 1)
                before = pltpu.roll(value, 1, 1)
                averaged = jnp.where(
                    (phase == 3) & (position < y_points - 1),
                    (value + after) * 0.5,
                    jnp.where((phase == 0) & (position > 0), (value + before) * 0.5, value),
                )
                couple(f, here, averaged)

    @pl.when(jnp.logical_not(atmosphere))
    def _():
        part = own_ref.shape[2]
        for f in range(3):
            couple(f, slice(0, part), helped_ref[f])
            couple(f, slice(part, 2 * part), own_ref[f])


def body(
    state, send_rows, intersection_source, intersection_weight, couple_rate, atm_metric, wave_speed,
    ocean_adjacent, ocean_edges, ocean_kappa,
):
    levels, rows = state.shape[1], state.shape[2]
    y_points = ocean_edges.shape[1]
    x_points = rows // y_points
    n = lax.axis_size("dom")
    sec = lax.axis_index("sec")
    slots = send_rows.shape[0]
    cap = slots // n
    part = rows // 2
    f32 = jnp.float32

    border = jax.ShapeDtypeStruct((3, levels, y_points), f32)
    whole = jax.ShapeDtypeStruct(state.shape, f32)
    arriving = jax.ShapeDtypeStruct((n, 3, cap // LANES, LANES), f32)
    incoming, stepped, west_a, east_a, west_o, east_o, ocean = pl.pallas_call(
        functools.partial(prepare_kernel, n, x_points, y_points),
        out_shape=[arriving, whole] + [border] * 4 + [whole],
        in_specs=[VMEM] * 2 + [SMEM, VMEM, SMEM],
        out_specs=[VMEM] * 7,
        scratch_shapes=[
            pltpu.VMEM((3 * rows // LANES, LANES), f32),
            pltpu.VMEM((3 * rows // LANES, 2 * LANES), jnp.bfloat16),
            pltpu.VMEM(arriving.shape, f32),
            pltpu.VMEM((3, levels, 2 * y_points), f32),
            pltpu.VMEM((rows, LANES), f32),
            pltpu.VMEM((2 * y_points, LANES), f32),
            pltpu.SemaphoreType.DMA((n,)),
            pltpu.SemaphoreType.DMA((n,)),
            pltpu.SemaphoreType.DMA((5,)),
            pltpu.SemaphoreType.DMA((5,)),
        ],
        compiler_params=pltpu.CompilerParams(collective_id=0, has_side_effects=True, **PARAMS),
        cost_estimate=pl.CostEstimate(
            flops=6 * rows * LANES * slots // LANES, bytes_accessed=3 * state.size * 4, transcendentals=0
        ),
        name="prepare",
    )(
        send_rows.reshape(-1, LANES),
        state,
        ocean_edges,
        atm_metric,
        wave_speed,
    )

    ocean = jnp.where(sec == 0, ocean, state)
    adjacent = lax.dynamic_slice_in_dim(ocean_adjacent, sec * part, part, 1).reshape(-1)
    swept, regrid = pl.pallas_call(
        sweep_kernel,
        out_shape=[jax.ShapeDtypeStruct((3, levels, part), f32), jax.ShapeDtypeStruct((3, rows), f32)],
        in_specs=[VMEM] * 3 + [SMEM] + [VMEM] * 4,
        out_specs=[VMEM] * 2,
        scratch_shapes=[
            pltpu.VMEM((rows + 2 * y_points, LANES), f32),
            pltpu.VMEM((part, LANES), f32),
            pltpu.VMEM((3 * slots // LANES, 2 * LANES), jnp.bfloat16),
            pltpu.VMEM((slots // LANES // 2, 2 * LANES), jnp.int32),
            pltpu.VMEM((slots // LANES // 2, 2 * LANES), f32),
        ],
        compiler_params=pltpu.CompilerParams(**PARAMS),
        name="sweep",
    )(
        ocean, west_o, east_o, adjacent, ocean_kappa.reshape(-1, LANES), incoming,
        intersection_source.reshape(-1, LANES), intersection_weight.reshape(-1, LANES),
    )
    helped = lax.ppermute(swept, "sec", [(0, 1)])

    return pl.pallas_call(
        functools.partial(finish_kernel, x_points, y_points),
        out_shape=jax.ShapeDtypeStruct(state.shape, f32),
        in_specs=[VMEM, SMEM] + [VMEM] * 5,
        out_specs=VMEM,
        compiler_params=pltpu.CompilerParams(**PARAMS),
        name="finish",
    )(regrid, couple_rate, stepped, west_a, east_a, swept, helped)


def solution(mesh):
    in_specs = (
        P(None, None, ("sec", "dom")),
        P(("sec", "dom")),
        P(("sec", "dom")),
        P(("sec", "dom")),
        P("sec", None),
        P(None, "dom"),
        P(),
        P(None, "dom"),
        P(None, "dom"),
        P("dom"),
    )
    out_specs = P(None, None, ("sec", "dom"))
    return jax.shard_map(body, mesh=mesh, in_specs=in_specs, out_specs=out_specs, check_vma=False)
```
